32 devices in a mesh: energy: 8 (over z, x), mom: 4 (over y, core).
Axes of the slice: x: 2, y: 2, z: 4, core: 2. Of those that a mesh axis runs over, the one named last changes fastest.
Arguments:
- inverse_blocks: bfloat16 [2, 16, 4, 2048, 256], P(None, 'energy', 'mom'), may hold values from -0.25 to 0.25
- coupling_blocks: bfloat16 [2, 4, 2048, 256], P(None, 'mom'), may hold values from -0.10595703 to 0.10595703
- shifts: int32 [4], replicated, may hold values from 0 to 1, as said below
- emission_weight: float32 [4, 4, 4], replicated, may hold values from 0.5 to 4
- absorption_weight: float32 [4, 4, 4], replicated, may hold values from 0.5 to 4
- deform_potential: float32 [2048], replicated, may hold values from 0.5 to 2
- range_rows: int32 [32], replicated, may hold values from 1 to 128, 2048 in all
Outputs:
- sigma: bfloat16 [2, 16, 4, 2048, 256], P(None, 'energy', 'mom')
- charge: float32 [32], P(('energy', 'mom'))
The draws below stay inside these ranges and needn't reach their ends.
Inputs may be any that keep to these rules, and one draw needn't show every extreme that they name: `shifts`: one mode's shift is exactly 1. `range_rows`: the counts add up to 2048; the largest is exactly 128.
All inputs are finite; a program needn't handle non-finite values.
Results may differ from the reference program's by a relative error of at most 0.015.
Values may be sent and summed in bfloat16 or wider, within the bound.
No kernel may reach another device: no remote copies, remote signals or barrier semaphores. Data moves between devices by JAX's collectives and lax.ppermute only.
A program may use at most 192 MiB of HBM per device.

```python
import math
import jax
import jax.numpy as jnp
import numpy as np
from jax import lax

B = 256
NB = 8
P_SIZE = 4
E = 16
K = 4
ROWS = 2048
ROWMAX = 128
SMAX = 1
DEVICES = 32


def draw_shifts(key, part):
    values = jax.random.randint(key, (P_SIZE,), 0, SMAX + 1)
    chosen = jax.random.randint(jax.random.fold_in(key, 7), (), 0, P_SIZE)
    return jnp.where(jnp.arange(P_SIZE) == chosen, SMAX, values).astype(jnp.int32)


def shard_levels(own_key, shape, pieces, least, high):
    loudness = 1.0
    for dim, shards_of in pieces:
        heights = jax.random.uniform(jax.random.fold_in(jax.random.fold_in(own_key, 6), dim), (shards_of,), jnp.float32, least / len(pieces), high / len(pieces))
        loudness = loudness * jnp.repeat(jnp.exp(heights), shape[dim] // shards_of).reshape((-1,) + (1,) * (len(shape) - 1 - dim))
    return loudness


def length_profile(number_of, total, most, lean):
    loads = [(1 << 20) // math.isqrt(standing ** lean) + 1 for standing in range(2, number_of + 1)]
    rest, holding = total - most - (number_of - 1), [1] * (number_of - 1)
    while rest > 0:
        candidates = [i for i in range(number_of - 1) if holding[i] < most]
        mass, budget = sum([loads[i] for i in candidates]), rest
        for i in candidates:
            addition = min(most - holding[i], max(1, budget * loads[i] // mass), rest)
            holding[i] = holding[i] + addition
            rest = rest - addition
    return np.array([most] + holding)


def ragged_sizes(key, amount, total, bound, lean):
    if amount == 2:
        one = jax.random.randint(key, (), max(1, total - bound), min(bound, total - 1) + 1)
        return jnp.stack([one, total - one])
    sizes = jnp.asarray(length_profile(amount, total, bound, lean), jnp.int32)
    pairs = (amount - 1) // 2
    donor, taker = sizes[1:1 + 2 * pairs:2], sizes[2:2 + 2 * pairs:2]
    room = jnp.minimum(donor - 1, bound - taker)
    moved = jax.random.randint(jax.random.fold_in(key, 1), (pairs,), 0, 1 << 20) % (room + 1)
    sizes = sizes.at[1:1 + 2 * pairs:2].set(donor - moved).at[2:2 + 2 * pairs:2].set(taker + moved)
    return sizes[jax.random.permutation(jax.random.fold_in(key, 2), amount)]


def normal_values(own_key, extent, deviation, limit, pieces=(), kind=jnp.bfloat16):
    level = shard_levels(own_key, extent, pieces, -0.22, 0.18) if pieces else 1.0
    entries = jax.random.normal(own_key, extent, jnp.float32) * deviation * level
    return jnp.minimum(jnp.maximum(entries, -limit), limit).astype(kind)


def setup_inputs(seed: int = 0) -> dict:
    splits = jax.random.split(jax.random.key(seed), 8)
    inverse_blocks = normal_values(splits[0], (2, E, K, ROWS, B), (2 * B) ** -0.5, 0.25, ((1, 8), (2, 4)))
    coupling_blocks = normal_values(splits[1], (2, K, ROWS, B), (0.4 / (2 * B) ** 0.5), 0.10595703, ((1, 4),))
    shifts = draw_shifts(jax.random.fold_in(splits[7], 71), 0)
    emission_weight = jnp.clip(jnp.exp(jax.random.uniform(splits[3], (P_SIZE, K, K), jnp.float32, math.log(0.5), math.log(4.0))), 0.5, 4.0)
    absorption_weight = jnp.clip(jnp.exp(jax.random.uniform(splits[4], (P_SIZE, K, K), jnp.float32, math.log(0.5), math.log(4.0))), 0.5, 4.0)
    deform_potential = jnp.clip(jnp.exp(jax.random.uniform(splits[5], (ROWS,), jnp.float32, math.log(0.5), math.log(2.0))), 0.5, 2.0)
    range_rows = ragged_sizes(splits[6], DEVICES, ROWS, ROWMAX, 2).astype(jnp.int32)
    return {"inverse_blocks": inverse_blocks, "coupling_blocks": coupling_blocks, "shifts": shifts, "emission_weight": emission_weight, "absorption_weight": absorption_weight, "deform_potential": deform_potential, "range_rows": range_rows}


HIGH = lax.Precision.HIGHEST


def rounded(value):
    return lax.optimization_barrier(value.astype(jnp.bfloat16)).astype(jnp.float32)


def complex_einsum(spec, left_re, left_im, right_re, right_im):
    def product(first, second):
        return jnp.einsum(spec, first, second, precision=HIGH)
    return (product(left_re, right_re) - product(left_im, right_im),
            product(left_re, right_im) + product(left_im, right_re))


def reference(inverse_blocks, coupling_blocks, shifts, emission_weight, absorption_weight, deform_potential, range_rows):
    inverse = inverse_blocks.astype(jnp.float32).reshape(2, E, K, NB, B, B)
    coupled = coupling_blocks.astype(jnp.float32).reshape(2, K, NB, B, B)
    row_parts = []
    sigma_parts = []
    green_re = None
    green_im = None
    for block in range(NB):
        a_re = inverse[0, :, :, block]
        a_im = inverse[1, :, :, block]
        t_re = coupled[0, :, block]
        t_im = coupled[1, :, block]
        if block == 0:
            s_re, s_im = complex_einsum('kij,klj->kil', t_re, t_im, t_re, -t_im)
            s_re = jnp.broadcast_to(rounded(s_re)[None], (E, K, B, B))
            s_im = jnp.broadcast_to(rounded(s_im)[None], (E, K, B, B))
        else:
            p_re, p_im = complex_einsum('kij,ekjl->ekil', t_re, t_im, green_re, green_im)
            p_re, p_im = rounded(p_re), rounded(p_im)
            s_re, s_im = complex_einsum('ekij,klj->ekil', p_re, p_im, t_re, -t_im)
            s_re, s_im = rounded(s_re), rounded(s_im)
        q_re, q_im = complex_einsum('ekij,ekjl->ekil', a_re, a_im, s_re, s_im)
        q_re, q_im = rounded(q_re), rounded(q_im)
        h_re, h_im = complex_einsum('ekij,ekjl->ekil', q_re, q_im, a_re, a_im)
        green_re = rounded(a_re + h_re)
        green_im = rounded(a_im + h_im)
        row_parts.append(-jnp.sum(jnp.diagonal(green_im, axis1=2, axis2=3), axis=(0, 1)))
        stacked = jnp.stack([green_re, green_im])
        padded = jnp.pad(stacked, ((0, 0), (SMAX, SMAX), (0, 0), (0, 0), (0, 0)))
        total = jnp.zeros((2, E, K, B, B), jnp.float32)
        for mode in range(P_SIZE):
            lower = lax.dynamic_slice_in_dim(padded, (SMAX - shifts[mode]).astype(jnp.int32), E, 1)
            upper = lax.dynamic_slice_in_dim(padded, (SMAX + shifts[mode]).astype(jnp.int32), E, 1)
            total = total + jnp.einsum('kq,zeqij->zekij', emission_weight[mode], lower, precision=HIGH)
            total = total + jnp.einsum('kq,zeqij->zekij', absorption_weight[mode], upper, precision=HIGH)
        scale = deform_potential[block * B:(block + 1) * B]
        sigma_parts.append((total * scale[:, None] * scale[None, :]).astype(jnp.bfloat16))
    sigma = jnp.stack(sigma_parts, axis=3).reshape(2, E, K, ROWS, B)
    density = jnp.concatenate(row_parts)
    starts = jnp.cumsum(range_rows) - range_rows
    row_ids = jnp.arange(ROWS, dtype=jnp.int32)
    member = (row_ids[:, None] >= starts[None, :]) & (row_ids[:, None] < (starts + range_rows)[None, :])
    charge = jnp.dot(density, member.astype(jnp.float32), precision=HIGH)
    return sigma, charge
```

```python
import functools

import jax
import jax.numpy as jnp
from jax import lax
from jax.experimental import pallas as pl
from jax.experimental.pallas import tpu as pltpu
from jax.sharding import PartitionSpec as P

CHUNKS = (("early", 0, 2), ("late", 2, 2), ("early", 4, 2), ("late", 6, 2))
VMEM = 63 * 2**20
TILE = 16
UNROLL = 4
ANY = pl.BlockSpec(memory_space=pltpu.HBM)
FACTOR = 100.0


def cost(us):
    return pl.CostEstimate(
        flops=int(us * FACTOR * 1.15e9), bytes_accessed=0, transcendentals=0
    )


F32 = jnp.float32
BF16 = jnp.bfloat16


def dot(left, right, transpose=False):
    dims = (((1,), (1 if transpose else 0,)), ((), ()))
    return lax.dot_general(left, right, dims, preferred_element_type=F32)


def complex_dot(left, right):
    re = dot(left[0], right[0]) - dot(left[1], right[1])
    im = dot(left[0], right[1]) + dot(left[1], right[0])
    return re.astype(BF16), im.astype(BF16)


def complex_dot_adjoint(left, right):
    re = dot(left[0], right[0], True) + dot(left[1], right[1], True)
    im = dot(left[1], right[0], True) - dot(left[0], right[1], True)
    return re.astype(BF16), im.astype(BF16)


def solve_kernel(first, edges, *refs):
    refs = list(refs)
    a_ref, t_ref = refs[:2]
    previous_ref = None if first else refs[2]
    carry = refs.pop()
    low_ref, high_ref = refs[-2:] if edges else (None, None)
    outs = refs[:-2] if edges else refs
    green_ref, density_ref = outs[-2:]
    energies = a_ref.shape[1]
    width = a_ref.shape[-1]
    t = (t_ref[0, 0], t_ref[1, 0])
    if not first:

        @pl.when(pl.program_id(0) == 0)
        def _():
            carry[...] = previous_ref[0]

    rows = lax.broadcasted_iota(jnp.int32, (width, width), 0)
    columns = lax.broadcasted_iota(jnp.int32, (width, width), 1)
    total = jnp.zeros((8, width), F32)
    if first:

        @pl.when(pl.program_id(0) == 0)
        def _():
            couple = complex_dot_adjoint(t, t)
            for e in range(energies):
                carry[0, e], carry[1, e] = couple

        @pl.when(pl.program_id(0) > 0)
        def _():
            for e in range(energies):
                left = complex_dot(t, (carry[0, e], carry[1, e]))
                carry[0, e], carry[1, e] = complex_dot_adjoint(left, t)

    for e in range(energies):
        a = (a_ref[0, e, 0], a_ref[1, e, 0])
        if first:
            couple = (carry[0, e], carry[1, e])
        else:
            left = complex_dot(t, (carry[0, e], carry[1, e]))
            couple = complex_dot_adjoint(left, t)
        inner = complex_dot(a, couple)
        re = a[0].astype(F32) + (dot(inner[0], a[0]) - dot(inner[1], a[1]))
        im = a[1].astype(F32) + (dot(inner[0], a[1]) + dot(inner[1], a[0]))
        re, im = re.astype(BF16), im.astype(BF16)
        carry[0, e] = re
        carry[1, e] = im
        green_ref[0, 0, e] = re
        green_ref[0, 1, e] = im
        if edges and e == 0:
            low_ref[0, 0] = re
            low_ref[0, 1] = im
        if edges and e == energies - 1:
            high_ref[0, 0] = re
            high_ref[0, 1] = im
        diagonal = jnp.where(rows == columns, im.astype(F32), 0.0)
        total = total + jnp.sum(diagonal.reshape(width // 8, 8, width), axis=0)
    density_ref[0] = total


def solve(inverse, coupled, previous, start, count, edges, after=()):
    _, energies, _, total_rows, width = inverse.shape
    first = previous is None
    args = [inverse, coupled]
    in_specs = [
        pl.BlockSpec((2, energies, 1, width, width), lambda i: (0, 0, 0, start + i, 0)),
        pl.BlockSpec((2, 1, width, width), lambda i: (0, 0, start + i, 0)),
    ]
    if not first:
        last = previous.shape[0] - 1
        args.append(previous)
        in_specs.append(
            pl.BlockSpec((1, 2, energies, width, width), lambda i: (last, 0, 0, 0, 0))
        )
    args.extend(after)
    in_specs.extend([ANY] * len(after))
    out_shape = [
        jax.ShapeDtypeStruct((count, 2, energies, width, width), BF16),
        jax.ShapeDtypeStruct((count, 8, width), F32),
    ]
    out_specs = [
        pl.BlockSpec((1, 2, energies, width, width), lambda i: (i, 0, 0, 0, 0)),
        pl.BlockSpec((1, 8, width), lambda i: (i, 0, 0)),
    ]
    if edges:
        for _ in range(2):
            out_shape.append(jax.ShapeDtypeStruct((count, 2, width, width), BF16))
            out_specs.append(pl.BlockSpec((1, 2, width, width), lambda i: (i, 0, 0, 0)))
    return pl.pallas_call(
        functools.partial(solve_kernel, first, edges),
        grid=(count,),
        in_specs=in_specs,
        out_specs=out_specs,
        out_shape=out_shape,
        scratch_shapes=[pltpu.VMEM((2, energies, width, width), BF16)],
        compiler_params=pltpu.CompilerParams(vmem_limit_bytes=VMEM),
        cost_estimate=cost(2.5 * count),
        name="solve",
    )(*args)


def grid_spec(energies, width):
    return pl.BlockSpec((1, 2, energies, width, width), lambda i: (i, 0, 0, 0, 0))


def edge_spec(width):
    return pl.BlockSpec((1, 2, width, width), lambda i: (i, 0, 0, 0))


def member_spec(which, energies, width):
    return pl.BlockSpec(
        (None, 1, 2, energies, width, width), lambda i: (which, i, 0, 0, 0, 0)
    )


def early_members(own, crossed, other):
    count, _, energies, width, _ = own.shape
    spec = grid_spec(energies, width)
    specs = [spec, member_spec(0, energies, width), spec, member_spec(1, energies, width)]
    return [own, other, crossed, other], specs


def late_members(own, before, behind, other):
    count, _, energies, width, _ = own.shape
    edge = edge_spec(width)
    specs = [grid_spec(energies, width), edge, edge, grid_spec(energies + 2, width)]
    return [own, before, behind, other], specs


def join_early_kernel(own_ref, crossed_ref, *refs):
    out_ref = refs[-1]
    out_ref[0] = own_ref[...]
    out_ref[1] = crossed_ref[...]


def join_late_kernel(own_ref, before_ref, behind_ref, *refs):
    out_ref = refs[-1]
    energies = own_ref.shape[2]
    for part in range(2):
        out_ref[0, part, 0] = before_ref[0, part]
        for e in range(energies):
            out_ref[0, part, e + 1] = own_ref[0, part, e]
        out_ref[0, part, energies + 1] = behind_ref[0, part]


def join_early(own, crossed, after):
    count, _, energies, width, _ = own.shape
    spec = grid_spec(energies, width)
    return pl.pallas_call(
        join_early_kernel,
        grid=(count,),
        in_specs=[spec, spec] + [ANY] * len(after),
        out_specs=pl.BlockSpec(
            (2, 1, 2, energies, width, width), lambda i: (0, i, 0, 0, 0, 0)
        ),
        out_shape=jax.ShapeDtypeStruct((2,) + own.shape, BF16),
        compiler_params=pltpu.CompilerParams(vmem_limit_bytes=VMEM),
        cost_estimate=cost(1.3 * count),
        name="join_early",
    )(own, crossed, *after)


def join_late(own, before, behind, after):
    count, _, energies, width, _ = own.shape
    edge = edge_spec(width)
    return pl.pallas_call(
        join_late_kernel,
        grid=(count,),
        in_specs=[grid_spec(energies, width), edge, edge] + [ANY] * len(after),
        out_specs=grid_spec(energies + 2, width),
        out_shape=jax.ShapeDtypeStruct((count, 2, energies + 2, width, width), BF16),
        compiler_params=pltpu.CompilerParams(vmem_limit_bytes=VMEM),
        cost_estimate=cost(1.3 * count),
        name="join_late",
    )(own, before, behind, *after)


def tiles(width):
    steps = width // TILE

    def run(step_body):
        for part in range(2):

            @pl.loop(0, steps, unroll=UNROLL)
            def _(step):
                step_body(part, pl.ds(pl.multiple_of(step * TILE, TILE), TILE))

    return run


def weighted(terms):
    total = None
    for weight, value in terms:
        term = value if weight is None else weight * value
        total = term if total is None else total + term
    return total


def early_edges_kernel(w_ref, *refs):
    grids, (high_ref, low_ref) = refs[:4], refs[-2:]
    last = grids[0].shape[2] - 1
    width = grids[0].shape[-1]
    above = [w_ref[0, 0, j] for j in range(4)]
    below = [w_ref[0, 2, j] for j in range(4)]

    @tiles(width)
    def _(part, rows):
        high = [(above[j], grids[j][0, part, last, rows, :].astype(F32)) for j in range(4)]
        low = [(below[j], grids[j][0, part, 0, rows, :].astype(F32)) for j in range(4)]
        high_ref[0, part, rows, :] = weighted(high).astype(BF16)
        low_ref[0, part, rows, :] = weighted(low).astype(BF16)


def early_edges(weights, members, after):
    args, specs = early_members(*members)
    count, _, energies, width, _ = args[0].shape
    edge = jax.ShapeDtypeStruct((count, 2, width, width), BF16)
    return pl.pallas_call(
        early_edges_kernel,
        grid=(count,),
        in_specs=[pl.BlockSpec(memory_space=pltpu.SMEM)] + specs + [ANY] * len(after),
        out_specs=[edge_spec(width)] * 2,
        out_shape=[edge, edge],
        compiler_params=pltpu.CompilerParams(vmem_limit_bytes=VMEM),
        cost_estimate=cost(1.7 * count),
        name="early_edges",
    )(weights, *args, *after)


def late_line(refs, part, rows):
    own, before, behind, other = refs
    energies = own.shape[2]
    mine = [before[0, part, rows, :]]
    mine += [own[0, part, e, rows, :] for e in range(energies)]
    mine += [behind[0, part, rows, :]]
    theirs = [other[0, part, e, rows, :] for e in range(energies + 2)]
    return [[value.astype(F32) for value in line] for line in (mine, theirs)]


def late_sum_kernel(w_ref, *refs):
    members, out_ref = refs[:4], refs[-1]
    energies, width = members[0].shape[2:4]
    w = [[w_ref[1, o, j] for j in range(2)] for o in range(3)]

    @tiles(width)
    def _(part, rows):
        line = late_line(members, part, rows)
        for e in range(energies):
            terms = [(w[o][j], line[j][e + o]) for j in range(2) for o in range(3)]
            out_ref[0, part, e, rows, :] = weighted(terms).astype(BF16)


def late_sum(weights, members, after):
    args, specs = late_members(*members)
    count, _, energies, width, _ = args[0].shape
    return pl.pallas_call(
        late_sum_kernel,
        grid=(count,),
        in_specs=[pl.BlockSpec(memory_space=pltpu.SMEM)] + specs + [ANY] * len(after),
        out_specs=grid_spec(energies, width),
        out_shape=jax.ShapeDtypeStruct(args[0].shape, BF16),
        compiler_params=pltpu.CompilerParams(vmem_limit_bytes=VMEM),
        cost_estimate=cost(1.8 * count),
        name="late_sum",
    )(weights, *args, *after)


def finish_kernel(late, w_ref, across_ref, down_ref, *refs):
    members, received, out_ref = refs[:4], refs[4 : 5 if late else 6], refs[-1]
    energies, width = members[0].shape[2:4]
    w = [[w_ref[0, o, j] for j in range(4)] for o in range(3)]
    across = across_ref[0]

    @tiles(width)
    def _(part, rows):
        scale = down_ref[rows, :] * across
        if late:
            line = late_line(members, part, rows)
        else:
            line = [
                [None] + [ref[0, part, e, rows, :].astype(F32) for e in range(energies)] + [None]
                for ref in members
            ]
        for e in range(energies):
            terms = [
                (w[o][j], line[j][e + o])
                for j in range(len(line))
                for o in range(3)
                if line[j][e + o] is not None
            ]
            if late:
                terms.append((None, received[0][0, part, e, rows, :].astype(F32)))
            if not late and e == 0:
                terms.append((None, received[0][0, part, rows, :].astype(F32)))
            if not late and e == energies - 1:
                terms.append((None, received[1][0, part, rows, :].astype(F32)))
            out_ref[part, e, 0, rows, :] = (weighted(terms) * scale).astype(BF16)


def finish(sigma, shape, start, weights, across, down, late, members, received, after):
    args, specs = late_members(*members) if late else early_members(*members)
    count, _, energies, width, _ = args[0].shape
    args = [weights, across, down, *args, *received, *after]
    in_specs = [
        pl.BlockSpec(memory_space=pltpu.SMEM),
        pl.BlockSpec((1, 1, width), lambda i: (start + i, 0, 0)),
        pl.BlockSpec((width, 1), lambda i: (start + i, 0)),
    ] + specs
    in_specs += [grid_spec(energies, width)] if late else [edge_spec(width)] * 2
    in_specs += [ANY] * len(after)
    aliases = {}
    if sigma is not None:
        aliases = {len(args): 0}
        args.append(sigma)
        in_specs.append(ANY)
    return pl.pallas_call(
        functools.partial(finish_kernel, late),
        grid=(count,),
        in_specs=in_specs,
        out_specs=pl.BlockSpec(
            (2, energies, 1, width, width), lambda i: (0, 0, 0, start + i, 0)
        ),
        out_shape=jax.ShapeDtypeStruct(shape, BF16),
        input_output_aliases=aliases,
        compiler_params=pltpu.CompilerParams(vmem_limit_bytes=VMEM),
        cost_estimate=cost(2.2 * count),
        name="finish",
    )(*args)


def range_parts_kernel(count, range_ref, *refs):
    densities, out_ref = refs[:count], refs[-1]
    width = densities[0].shape[-1]
    lanes = lax.broadcasted_iota(jnp.int32, (8, 128), 1)
    pieces = []
    base = 0
    for ref in densities:
        for i in range(ref.shape[0]):
            for half in range(width // 128):
                pieces.append((base, ref[i, :, half * 128 : (half + 1) * 128]))
                base += 128

    def one_range(d, begin):
        end = begin + range_ref[d]
        total = jnp.zeros((8, 128), F32)
        for offset, value in pieces:
            inside = (lanes >= begin - offset) & (lanes < end - offset)
            total = total + jnp.where(inside, value, 0.0)
        out_ref[d] = -total
        return end

    lax.fori_loop(0, out_ref.shape[0], one_range, jnp.int32(0))


def range_parts(range_rows, densities, after):
    devices = range_rows.shape[0]
    return pl.pallas_call(
        functools.partial(range_parts_kernel, len(densities)),
        in_specs=[pl.BlockSpec(memory_space=pltpu.SMEM)]
        + [pl.BlockSpec(memory_space=pltpu.VMEM)] * len(densities)
        + [ANY] * len(after),
        out_specs=pl.BlockSpec(memory_space=pltpu.VMEM),
        out_shape=jax.ShapeDtypeStruct((devices, 8, 128), F32),
        compiler_params=pltpu.CompilerParams(vmem_limit_bytes=VMEM),
        cost_estimate=cost(2.2),
        name="range_parts",
    )(range_rows, *densities, *after)


def range_total_kernel(parts_ref, *refs):
    out_ref = refs[-1]
    out_ref[...] = jnp.sum(parts_ref[...], axis=0)


def range_total(received, after):
    return pl.pallas_call(
        range_total_kernel,
        in_specs=[pl.BlockSpec(memory_space=pltpu.VMEM)] + [ANY] * len(after),
        out_specs=pl.BlockSpec(memory_space=pltpu.VMEM),
        out_shape=jax.ShapeDtypeStruct(received.shape[1:], F32),
        compiler_params=pltpu.CompilerParams(vmem_limit_bytes=VMEM),
        cost_estimate=cost(1),
        name="range_total",
    )(received, *after)


def own_weights(shifts, emission, absorption):
    me = lax.axis_index("mom")
    folded = []
    for offset in (-1, 0, 1):
        lower = (shifts == -offset).astype(F32)[:, None, None]
        upper = (shifts == offset).astype(F32)[:, None, None]
        folded.append(jnp.sum(lower * emission + upper * absorption, axis=0))
    folded = jnp.stack(folded)
    momenta = jnp.arange(4, dtype=jnp.int32)
    targets = ((me ^ jnp.array([0, 2], jnp.int32))[:, None] == momenta[None]).astype(F32)
    sources = ((me ^ momenta)[:, None] == momenta[None]).astype(F32)
    picked = folded[None, :, None] * targets[:, None, None, :, None] * sources[None, None, :, None, :]
    return jnp.sum(picked, axis=(3, 4))


def body(
    inverse_blocks,
    coupling_blocks,
    shifts,
    emission_weight,
    absorption_weight,
    deform_potential,
    range_rows,
):
    n_energy = lax.axis_size("energy")
    width = inverse_blocks.shape[-1]
    up = [(i, i + 1) for i in range(n_energy - 1)]
    down = [(i + 1, i) for i in range(n_energy - 1)]

    def send(value, axis, pairs, name):
        with jax.named_scope(name):
            return lax.ppermute(value, axis, pairs)

    def core(value, name):
        return send(value, "mom", [(i, i ^ 1) for i in range(4)], name)

    def pair(value, name):
        return send(value, "mom", [(i, i ^ 2) for i in range(4)], name)

    def halo(low, high, name):
        return (
            send(high, "energy", up, "up" + name),
            send(low, "energy", down, "down" + name),
        )

    weights = own_weights(shifts, emission_weight, absorption_weight)
    across_scale = deform_potential.reshape(-1, 1, width)
    down_scale = deform_potential.reshape(-1, 1)

    def run(chunk, previous, after=()):
        kind, start, count = CHUNKS[chunk]
        return solve(
            inverse_blocks, coupling_blocks, previous, start, count, kind == "late", after
        )

    g0, n0 = run(0, None)
    y0 = pair(g0, "pair0")
    g1, n1, low1, high1 = run(1, g0)
    edges1 = halo(low1, high1, "1")
    g2, n2 = run(2, g1)
    y2 = pair(g2, "pair2")
    g3, n3, low3, high3 = run(3, g2)
    edges3 = halo(low3, high3, "3")
    j0 = join_early(g0, y0, (g3,))
    k0 = core(j0, "core0")
    j1 = join_late(g1, *edges1, (j0,))
    k1 = core(j1, "core1")
    members0 = (g0, y0, k0)
    high0, low0 = early_edges(weights, members0, (j1,))
    members1 = (g1, *edges1, k1)
    total1 = late_sum(weights, members1, (low0,))
    x1 = pair(total1, "pair1")
    edges0 = halo(low0, high0, "0")

    j2 = join_early(g2, y2, (total1,))
    k2 = core(j2, "core2")
    j3 = join_late(g3, *edges3, (j2,))
    k3 = core(j3, "core3")
    members2 = (g2, y2, k2)
    high2, low2 = early_edges(weights, members2, (j3,))
    members3 = (g3, *edges3, k3)
    total3 = late_sum(weights, members3, (low2,))
    x3 = pair(total3, "pair3")
    edges2 = halo(low2, high2, "2")

    parts = range_parts(range_rows, [n0, n1, n2, n3], (total3,))
    received = lax.all_to_all(parts, ("energy", "mom"), split_axis=0, concat_axis=0, tiled=True)
    charge = range_total(received, (x3,))

    sigma = None
    for index, late, members, got, after in (
        (1, True, members1, (x1,), (parts,)),
        (0, False, members0, edges0, ()),
        (3, True, members3, (x3,), ()),
        (2, False, members2, edges2, (charge,)),
    ):
        sigma = finish(
            sigma,
            inverse_blocks.shape,
            CHUNKS[index][1],
            weights,
            across_scale,
            down_scale,
            late,
            members,
            got,
            after,
        )
    return sigma, jnp.sum(charge).reshape(1)


def solution(mesh):
    in_specs = (
        P(None, "energy", "mom", None, None),
        P(None, "mom", None, None),
        P(),
        P(),
        P(),
        P(),
        P(),
    )
    out_specs = (P(None, "energy", "mom", None, None), P(("energy", "mom")))
    return jax.shard_map(body, mesh=mesh, in_specs=in_specs, out_specs=out_specs, check_vma=False)
```

```python
import functools

import jax
import jax.numpy as jnp
from jax import lax
from jax.experimental import pallas as pl
from jax.experimental.pallas import tpu as pltpu
from jax.sharding import PartitionSpec as P

CHUNKS = (("early", 0, 2), ("late", 2, 2), ("early", 4, 2), ("late", 6, 2))
VMEM = 63 * 2**20
TILE = 16
UNROLL = 4
ANY = pl.BlockSpec(memory_space=pltpu.HBM)
FACTOR = 100.0


def cost(us):
    return pl.CostEstimate(
        flops=int(us * FACTOR * 1.15e9), bytes_accessed=0, transcendentals=0
    )


F32 = jnp.float32
BF16 = jnp.bfloat16


def dot(left, right, transpose=False):
    dims = (((1,), (1 if transpose else 0,)), ((), ()))
    return lax.dot_general(left, right, dims, preferred_element_type=F32)


def complex_dot(left, right):
    wide = jnp.concatenate(left, axis=1)
    re = dot(wide, jnp.concatenate([right[0], -right[1]], axis=0))
    im = dot(wide, jnp.concatenate([right[1], right[0]], axis=0))
    return re.astype(BF16), im.astype(BF16)


def complex_dot_adjoint(left, right):
    wide = jnp.concatenate(left, axis=1)
    re = dot(wide, jnp.concatenate([right[0], right[1]], axis=1), True)
    im = dot(wide, jnp.concatenate([-right[1], right[0]], axis=1), True)
    return re.astype(BF16), im.astype(BF16)


def solve_kernel(first, edges, again, *refs):
    refs = list(refs)
    a_ref, t_ref = refs[:2]
    previous_ref = None if first else refs[2]
    carry = refs.pop()
    again_ref = refs.pop() if again else None
    low_ref, high_ref = refs[-2:] if edges else (None, None)
    outs = refs[:-2] if edges else refs
    green_ref, density_ref = outs[-2:]
    energies = a_ref.shape[1]
    width = a_ref.shape[-1]
    t = (t_ref[0, 0], t_ref[1, 0])
    if not first:

        @pl.when(pl.program_id(0) == 0)
        def _():
            carry[...] = previous_ref[0]

    rows = lax.broadcasted_iota(jnp.int32, (width, width), 0)
    columns = lax.broadcasted_iota(jnp.int32, (width, width), 1)
    total = jnp.zeros((8, width), F32)
    if first:

        @pl.when(pl.program_id(0) == 0)
        def _():
            couple = complex_dot_adjoint(t, t)
            for e in range(energies):
                carry[0, e], carry[1, e] = couple

        @pl.when(pl.program_id(0) > 0)
        def _():
            for e in range(energies):
                left = complex_dot(t, (carry[0, e], carry[1, e]))
                carry[0, e], carry[1, e] = complex_dot_adjoint(left, t)

    blocks = [(a_ref[0, e, 0], a_ref[1, e, 0]) for e in range(energies)]
    couples = [(carry[0, e], carry[1, e]) for e in range(energies)]
    if not first:
        lefts = [complex_dot(t, green) for green in couples]
        couples = [complex_dot_adjoint(left, t) for left in lefts]
    inners = [complex_dot(a, couple) for a, couple in zip(blocks, couples)]
    for e in range(energies):
        a, inner = blocks[e], inners[e]
        wide = jnp.concatenate(inner, axis=1)
        re = a[0].astype(F32) + dot(wide, jnp.concatenate([a[0], -a[1]], axis=0))
        im = a[1].astype(F32) + dot(wide, jnp.concatenate([a[1], a[0]], axis=0))
        re, im = re.astype(BF16), im.astype(BF16)
        carry[0, e] = re
        carry[1, e] = im
        green_ref[0, 0, e] = re
        green_ref[0, 1, e] = im
        if again:
            again_ref[0, 0, e] = re
            again_ref[0, 1, e] = im
        if edges and e == 0:
            low_ref[0, 0] = re
            low_ref[0, 1] = im
        if edges and e == energies - 1:
            high_ref[0, 0] = re
            high_ref[0, 1] = im
        diagonal = jnp.where(rows == columns, im.astype(F32), 0.0)
        total = total + jnp.sum(diagonal.reshape(width // 8, 8, width), axis=0)
    density_ref[0] = total


def solve(inverse, coupled, previous, start, count, edges, again, after=()):
    _, energies, _, total_rows, width = inverse.shape
    first = previous is None
    args = [inverse, coupled]
    in_specs = [
        pl.BlockSpec((2, energies, 1, width, width), lambda i: (0, 0, 0, start + i, 0)),
        pl.BlockSpec((2, 1, width, width), lambda i: (0, 0, start + i, 0)),
    ]
    if not first:
        last = previous.shape[0] - 1
        args.append(previous)
        in_specs.append(
            pl.BlockSpec((1, 2, energies, width, width), lambda i: (last, 0, 0, 0, 0))
        )
    args.extend(after)
    in_specs.extend([ANY] * len(after))
    out_shape = [
        jax.ShapeDtypeStruct((count, 2, energies, width, width), BF16),
        jax.ShapeDtypeStruct((count, 8, width), F32),
    ]
    out_specs = [
        pl.BlockSpec((1, 2, energies, width, width), lambda i: (i, 0, 0, 0, 0)),
        pl.BlockSpec((1, 8, width), lambda i: (i, 0, 0)),
    ]
    if edges:
        for _ in range(2):
            out_shape.append(jax.ShapeDtypeStruct((count, 2, width, width), BF16))
            out_specs.append(pl.BlockSpec((1, 2, width, width), lambda i: (i, 0, 0, 0)))
    if again:
        out_shape.append(out_shape[0])
        out_specs.append(out_specs[0])
    return pl.pallas_call(
        functools.partial(solve_kernel, first, edges, again),
        grid=(count,),
        in_specs=in_specs,
        out_specs=out_specs,
        out_shape=out_shape,
        scratch_shapes=[pltpu.VMEM((2, energies, width, width), BF16)],
        compiler_params=pltpu.CompilerParams(vmem_limit_bytes=VMEM),
        cost_estimate=cost(2.5 * count),
        name="solve",
    )(*args)


def grid_spec(energies, width):
    return pl.BlockSpec((1, 2, energies, width, width), lambda i: (i, 0, 0, 0, 0))


def edge_spec(width):
    return pl.BlockSpec((1, 2, width, width), lambda i: (i, 0, 0, 0))


def early_members(*blocks):
    count, _, energies, width, _ = blocks[0].shape
    return list(blocks), [grid_spec(energies, width)] * 4


def late_members(own, other, *edges):
    count, _, energies, width, _ = own.shape
    specs = [grid_spec(energies, width)] * 2 + [edge_spec(width)] * 4
    return [own, other, *edges], specs


def gate_kernel(*refs):
    pass


def gate(values, after):
    count = len(values)
    return pl.pallas_call(
        gate_kernel,
        in_specs=[ANY] * (count + len(after)),
        out_specs=[ANY] * count,
        out_shape=[jax.ShapeDtypeStruct(value.shape, value.dtype) for value in values],
        input_output_aliases={i: i for i in range(count)},
        compiler_params=pltpu.CompilerParams(vmem_limit_bytes=VMEM),
        cost_estimate=cost(2.0),
        name="gate",
    )(*values, *after)


def tiles(width):
    steps = width // TILE

    def run(step_body):
        for part in range(2):

            @pl.loop(0, steps, unroll=UNROLL)
            def _(step):
                step_body(part, pl.ds(pl.multiple_of(step * TILE, TILE), TILE))

    return run


def weighted(terms):
    total = None
    for weight, value in terms:
        term = value if weight is None else weight * value
        total = term if total is None else total + term
    return total


def early_edges_kernel(w_ref, *refs):
    grids, (high_ref, low_ref) = refs[:4], refs[-2:]
    last = grids[0].shape[2] - 1
    width = grids[0].shape[-1]
    above = [w_ref[0, 0, j] for j in range(4)]
    below = [w_ref[0, 2, j] for j in range(4)]

    @tiles(width)
    def _(part, rows):
        high = [(above[j], grids[j][0, part, last, rows, :].astype(F32)) for j in range(4)]
        low = [(below[j], grids[j][0, part, 0, rows, :].astype(F32)) for j in range(4)]
        high_ref[0, part, rows, :] = weighted(high).astype(BF16)
        low_ref[0, part, rows, :] = weighted(low).astype(BF16)


def early_edges(weights, members, after):
    args, specs = early_members(*members)
    count, _, energies, width, _ = args[0].shape
    edge = jax.ShapeDtypeStruct((count, 2, width, width), BF16)
    return pl.pallas_call(
        early_edges_kernel,
        grid=(count,),
        in_specs=[pl.BlockSpec(memory_space=pltpu.SMEM)] + specs + [ANY] * len(after),
        out_specs=[edge_spec(width)] * 2,
        out_shape=[edge, edge],
        compiler_params=pltpu.CompilerParams(vmem_limit_bytes=VMEM),
        cost_estimate=cost(1.7 * count),
        name="early_edges",
    )(weights, *args, *after)


def late_line(refs, part, rows):
    grids, edges = refs[:2], refs[2:]
    lines = []
    for j in range(2):
        line = [edges[2 * j][0, part, rows, :]]
        line += [grids[j][0, part, e, rows, :] for e in range(grids[j].shape[2])]
        line += [edges[2 * j + 1][0, part, rows, :]]
        lines.append([value.astype(F32) for value in line])
    return lines


def late_sum_kernel(w_ref, *refs):
    members, out_ref = refs[:6], refs[-1]
    energies, width = members[0].shape[2:4]
    w = [[w_ref[1, o, j] for j in range(2)] for o in range(3)]

    @tiles(width)
    def _(part, rows):
        line = late_line(members, part, rows)
        for e in range(energies):
            terms = [(w[o][j], line[j][e + o]) for j in range(2) for o in range(3)]
            out_ref[0, part, e, rows, :] = weighted(terms).astype(BF16)


def late_sum(weights, members, after):
    args, specs = late_members(*members)
    count, _, energies, width, _ = args[0].shape
    return pl.pallas_call(
        late_sum_kernel,
        grid=(count,),
        in_specs=[pl.BlockSpec(memory_space=pltpu.SMEM)] + specs + [ANY] * len(after),
        out_specs=grid_spec(energies, width),
        out_shape=jax.ShapeDtypeStruct(args[0].shape, BF16),
        compiler_params=pltpu.CompilerParams(vmem_limit_bytes=VMEM),
        cost_estimate=cost(1.8 * count),
        name="late_sum",
    )(weights, *args, *after)


def finish_kernel(late, w_ref, across_ref, down_ref, *refs):
    members, received, out_ref = refs[: 6 if late else 4], refs[6:7] if late else refs[4:6], refs[-1]
    energies, width = members[0].shape[2:4]
    w = [[w_ref[0, o, j] for j in range(4)] for o in range(3)]
    across = across_ref[0]

    @tiles(width)
    def _(part, rows):
        scale = down_ref[rows, :] * across
        if late:
            line = late_line(members, part, rows)
        else:
            line = [
                [None] + [ref[0, part, e, rows, :].astype(F32) for e in range(energies)] + [None]
                for ref in members
            ]
        for e in range(energies):
            terms = [
                (w[o][j], line[j][e + o])
                for j in range(len(line))
                for o in range(3)
                if line[j][e + o] is not None
            ]
            if late:
                terms.append((None, received[0][0, part, e, rows, :].astype(F32)))
            if not late and e == 0:
                terms.append((None, received[0][0, part, rows, :].astype(F32)))
            if not late and e == energies - 1:
                terms.append((None, received[1][0, part, rows, :].astype(F32)))
            out_ref[part, e, 0, rows, :] = (weighted(terms) * scale).astype(BF16)


def finish(sigma, shape, start, weights, across, down, late, members, received, after):
    args, specs = late_members(*members) if late else early_members(*members)
    count, _, energies, width, _ = args[0].shape
    args = [weights, across, down, *args, *received, *after]
    in_specs = [
        pl.BlockSpec(memory_space=pltpu.SMEM),
        pl.BlockSpec((1, 1, width), lambda i: (start + i, 0, 0)),
        pl.BlockSpec((width, 1), lambda i: (start + i, 0)),
    ] + specs
    in_specs += [grid_spec(energies, width)] if late else [edge_spec(width)] * 2
    in_specs += [ANY] * len(after)
    aliases = {}
    if sigma is not None:
        aliases = {len(args): 0}
        args.append(sigma)
        in_specs.append(ANY)
    return pl.pallas_call(
        functools.partial(finish_kernel, late),
        grid=(count,),
        in_specs=in_specs,
        out_specs=pl.BlockSpec(
            (2, energies, 1, width, width), lambda i: (0, 0, 0, start + i, 0)
        ),
        out_shape=jax.ShapeDtypeStruct(shape, BF16),
        input_output_aliases=aliases,
        compiler_params=pltpu.CompilerParams(vmem_limit_bytes=VMEM),
        cost_estimate=cost(2.2 * count),
        name="finish",
    )(*args)


def range_parts_kernel(count, range_ref, *refs):
    densities, out_ref = refs[:count], refs[-1]
    width = densities[0].shape[-1]
    lanes = lax.broadcasted_iota(jnp.int32, (8, 128), 1)
    pieces = []
    base = 0
    for ref in densities:
        for i in range(ref.shape[0]):
            for half in range(width // 128):
                pieces.append((base, ref[i, :, half * 128 : (half + 1) * 128]))
                base += 128

    def one_range(d, begin):
        end = begin + range_ref[d]
        total = jnp.zeros((8, 128), F32)
        for offset, value in pieces:
            inside = (lanes >= begin - offset) & (lanes < end - offset)
            total = total + jnp.where(inside, value, 0.0)
        out_ref[d] = -total
        return end

    lax.fori_loop(0, out_ref.shape[0], one_range, jnp.int32(0))


def range_parts(range_rows, densities, after):
    devices = range_rows.shape[0]
    return pl.pallas_call(
        functools.partial(range_parts_kernel, len(densities)),
        in_specs=[pl.BlockSpec(memory_space=pltpu.SMEM)]
        + [pl.BlockSpec(memory_space=pltpu.VMEM)] * len(densities)
        + [ANY] * len(after),
        out_specs=pl.BlockSpec(memory_space=pltpu.VMEM),
        out_shape=jax.ShapeDtypeStruct((devices, 8, 128), F32),
        compiler_params=pltpu.CompilerParams(vmem_limit_bytes=VMEM),
        cost_estimate=cost(2.2),
        name="range_parts",
    )(range_rows, *densities, *after)


def range_total_kernel(parts_ref, *refs):
    out_ref = refs[-1]
    out_ref[0] = jnp.sum(parts_ref[...])


def range_total(received, after):
    return pl.pallas_call(
        range_total_kernel,
        in_specs=[pl.BlockSpec(memory_space=pltpu.VMEM)] + [ANY] * len(after),
        out_specs=pl.BlockSpec(memory_space=pltpu.SMEM),
        out_shape=jax.ShapeDtypeStruct((1,), F32),
        compiler_params=pltpu.CompilerParams(vmem_limit_bytes=VMEM),
        cost_estimate=cost(1),
        name="range_total",
    )(received, *after)


def own_weights(shifts, emission, absorption):
    me = lax.axis_index("mom")
    folded = []
    for offset in (-1, 0, 1):
        lower = (shifts == -offset).astype(F32)[:, None, None]
        upper = (shifts == offset).astype(F32)[:, None, None]
        folded.append(jnp.sum(lower * emission + upper * absorption, axis=0))
    folded = jnp.stack(folded)
    momenta = jnp.arange(4, dtype=jnp.int32)
    targets = ((me ^ jnp.array([0, 2], jnp.int32))[:, None] == momenta[None]).astype(F32)
    sources = ((me ^ momenta)[:, None] == momenta[None]).astype(F32)
    picked = folded[None, :, None] * targets[:, None, None, :, None] * sources[None, None, :, None, :]
    return jnp.sum(picked, axis=(3, 4))


def body(
    inverse_blocks,
    coupling_blocks,
    shifts,
    emission_weight,
    absorption_weight,
    deform_potential,
    range_rows,
):
    n_energy = lax.axis_size("energy")
    width = inverse_blocks.shape[-1]
    up = [(i, i + 1) for i in range(n_energy - 1)]
    down = [(i + 1, i) for i in range(n_energy - 1)]

    def send(value, axis, pairs, name):
        with jax.named_scope(name):
            return lax.ppermute(value, axis, pairs)

    def core(value, name):
        return send(value, "mom", [(i, i ^ 1) for i in range(4)], name)

    def pair(value, name):
        return send(value, "mom", [(i, i ^ 2) for i in range(4)], name)

    weights = own_weights(shifts, emission_weight, absorption_weight)
    across_scale = deform_potential.reshape(-1, 1, width)
    down_scale = deform_potential.reshape(-1, 1)

    def run(chunk, previous, after=(), again=False):
        kind, start, count = CHUNKS[chunk]
        return solve(
            inverse_blocks, coupling_blocks, previous, start, count, kind == "late", again, after
        )

    def rise(value, name):
        return send(value, "energy", up, "up" + name)

    def fall(value, name):
        return send(value, "energy", down, "down" + name)

    def done(sigma, chunk, members, got, after=()):
        kind, start, _ = CHUNKS[chunk]
        return finish(
            sigma,
            inverse_blocks.shape,
            start,
            weights,
            across_scale,
            down_scale,
            kind == "late",
            members,
            got,
            after,
        )

    g0, n0 = run(0, None)
    y0, c0 = pair(g0, "pair0"), core(g0, "core0")
    g1, n1, low1, high1 = run(1, g0)
    up1, down1, c1 = rise(high1, "1"), fall(low1, "1"), core(g1, "core1")
    g2, n2, h2 = run(2, g1, (c0,), True)
    y2 = pair(g2, "pair2")
    g3, n3, low3, high3, h3 = run(3, g2, (c1,), True)

    (y0,) = gate([y0], (g3,))
    core_y0 = core(y0, "core_pair0")
    (c0,) = gate([c0], (y0,))
    members0 = (g0, c0, y0, core_y0)
    high0, low0 = early_edges(weights, members0, ())

    low3, high3, h3 = gate([low3, high3, h3], (low0,))
    up3, down3, c3 = rise(high3, "3"), fall(low3, "3"), core(h3, "core3")
    (n0,) = gate([n0], (low3,))

    up1, down1 = gate([up1, down1], (n0, c3))
    core_up1, core_down1 = core(up1, "core_up1"), core(down1, "core_down1")
    (c1,) = gate([c1], (up1,))
    members1 = (g1, c1, up1, down1, core_up1, core_down1)
    total1 = late_sum(weights, members1, ())
    x1 = pair(total1, "pair1")

    y2, high0, low0, h2 = gate([y2, high0, low0, h2], (total1,))
    up0, down0, c2 = rise(high0, "0"), fall(low0, "0"), core(h2, "core2")

    (n1,) = gate([n1], (y2,))
    parts = range_parts(range_rows, [n0, n1, n2, n3], (c2,))
    received = lax.all_to_all(parts, ("energy", "mom"), split_axis=0, concat_axis=0, tiled=True)

    (y2,) = gate([y2], (parts,))
    core_y2 = core(y2, "core_pair2")
    (c2,) = gate([c2], (y2,))
    members2 = (g2, c2, y2, core_y2)
    high2, low2 = early_edges(weights, members2, ())

    up3, down3 = gate([up3, down3], (low2,))
    core_up3, core_down3 = core(up3, "core_up3"), core(down3, "core_down3")
    (c3,) = gate([c3], (up3,))
    members3 = (g3, c3, up3, down3, core_up3, core_down3)
    total3 = late_sum(weights, members3, ())
    x3 = pair(total3, "pair3")
    x1, high2, low2 = gate([x1, high2, low2], (total3,))
    up2, down2 = rise(high2, "2"), fall(low2, "2")

    sigma = done(None, 1, members1, (x1,))
    sigma = done(sigma, 0, members0, (up0, down0))
    charge = range_total(received, (sigma,))
    sigma = done(sigma, 3, members3, (x3,), (charge,))
    sigma = done(sigma, 2, members2, (up2, down2))
    return sigma, charge


def solution(mesh):
    in_specs = (
        P(None, "energy", "mom", None, None),
        P(None, "mom", None, None),
        P(),
        P(),
        P(),
        P(),
        P(),
    )
    out_specs = (P(None, "energy", "mom", None, None), P(("energy", "mom")))
    return jax.shard_map(body, mesh=mesh, in_specs=in_specs, out_specs=out_specs, check_vma=False)
```

```python
import functools

import jax
import jax.numpy as jnp
from jax import lax
from jax.experimental import pallas as pl
from jax.experimental.pallas import tpu as pltpu
from jax.sharding import PartitionSpec as P

CHUNKS = (("late", 0, 2), ("early", 2, 2), ("late", 4, 2), ("early", 6, 2))
VMEM = 63 * 2**20
TILE = 16
UNROLL = 4
ANY = pl.BlockSpec(memory_space=pltpu.HBM)
LOOSE = pl.BlockSpec(memory_space=pl.ANY)
FACTOR = 100.0


def cost(us):
    return pl.CostEstimate(
        flops=int(us * FACTOR * 1.15e9), bytes_accessed=0, transcendentals=0
    )


F32 = jnp.float32
BF16 = jnp.bfloat16


def unread(values):
    return [ANY if value.size > 2**16 else LOOSE for value in values]


def dot(left, right, transpose=False):
    dims = (((1,), (1 if transpose else 0,)), ((), ()))
    return lax.dot_general(left, right, dims, preferred_element_type=F32)


def complex_dot(left, right):
    wide = jnp.concatenate(left, axis=1)
    re = dot(wide, jnp.concatenate([right[0], -right[1]], axis=0))
    im = dot(wide, jnp.concatenate([right[1], right[0]], axis=0))
    return re.astype(BF16), im.astype(BF16)


def complex_dot_adjoint(left, right):
    wide = jnp.concatenate(left, axis=1)
    re = dot(wide, jnp.concatenate([right[0], right[1]], axis=1), True)
    im = dot(wide, jnp.concatenate([-right[1], right[0]], axis=1), True)
    return re.astype(BF16), im.astype(BF16)


def solve_kernel(first, edges, again, *refs):
    refs = list(refs)
    a_ref, t_ref = refs[:2]
    previous_ref = None if first else refs[2]
    carry = refs.pop()
    again_ref = refs.pop() if again else None
    low_ref, high_ref = refs[-2:] if edges else (None, None)
    outs = refs[:-2] if edges else refs
    green_ref, density_ref = outs[-2:]
    energies = a_ref.shape[1]
    width = a_ref.shape[-1]
    t = (t_ref[0, 0], t_ref[1, 0])
    if not first:

        @pl.when(pl.program_id(0) == 0)
        def _():
            carry[...] = previous_ref[0]

    rows = lax.broadcasted_iota(jnp.int32, (width, width), 0)
    columns = lax.broadcasted_iota(jnp.int32, (width, width), 1)
    total = jnp.zeros((8, width), F32)
    if first:

        @pl.when(pl.program_id(0) == 0)
        def _():
            couple = complex_dot_adjoint(t, t)
            for e in range(energies):
                carry[0, e], carry[1, e] = couple

        @pl.when(pl.program_id(0) > 0)
        def _():
            for e in range(energies):
                left = complex_dot(t, (carry[0, e], carry[1, e]))
                carry[0, e], carry[1, e] = complex_dot_adjoint(left, t)

    blocks = [(a_ref[0, e, 0], a_ref[1, e, 0]) for e in range(energies)]
    couples = [(carry[0, e], carry[1, e]) for e in range(energies)]
    if not first:
        lefts = [complex_dot(t, green) for green in couples]
        couples = [complex_dot_adjoint(left, t) for left in lefts]
    inners = [complex_dot(a, couple) for a, couple in zip(blocks, couples)]
    for e in range(energies):
        a, inner = blocks[e], inners[e]
        wide = jnp.concatenate(inner, axis=1)
        re = a[0].astype(F32) + dot(wide, jnp.concatenate([a[0], -a[1]], axis=0))
        im = a[1].astype(F32) + dot(wide, jnp.concatenate([a[1], a[0]], axis=0))
        re, im = re.astype(BF16), im.astype(BF16)
        carry[0, e] = re
        carry[1, e] = im
        green_ref[0, 0, e] = re
        green_ref[0, 1, e] = im
        if again:
            again_ref[0, 0, e] = re
            again_ref[0, 1, e] = im
        if edges and e == 0:
            low_ref[0, 0] = re
            low_ref[0, 1] = im
        if edges and e == energies - 1:
            high_ref[0, 0] = re
            high_ref[0, 1] = im
        diagonal = jnp.where(rows == columns, im.astype(F32), 0.0)
        total = total + jnp.sum(diagonal.reshape(width // 8, 8, width), axis=0)
    density_ref[0] = total


def solve(inverse, coupled, previous, start, count, edges, again, after=()):
    _, energies, _, total_rows, width = inverse.shape
    first = previous is None
    args = [inverse, coupled]
    in_specs = [
        pl.BlockSpec((2, energies, 1, width, width), lambda i: (0, 0, 0, start + i, 0)),
        pl.BlockSpec((2, 1, width, width), lambda i: (0, 0, start + i, 0)),
    ]
    if not first:
        last = previous.shape[0] - 1
        args.append(previous)
        in_specs.append(
            pl.BlockSpec((1, 2, energies, width, width), lambda i: (last, 0, 0, 0, 0))
        )
    args.extend(after)
    in_specs.extend(unread(after))
    out_shape = [
        jax.ShapeDtypeStruct((count, 2, energies, width, width), BF16),
        jax.ShapeDtypeStruct((count, 8, width), F32),
    ]
    out_specs = [
        pl.BlockSpec((1, 2, energies, width, width), lambda i: (i, 0, 0, 0, 0)),
        pl.BlockSpec((1, 8, width), lambda i: (i, 0, 0)),
    ]
    if edges:
        for _ in range(2):
            out_shape.append(jax.ShapeDtypeStruct((count, 2, width, width), BF16))
            out_specs.append(pl.BlockSpec((1, 2, width, width), lambda i: (i, 0, 0, 0)))
    if again:
        out_shape.append(out_shape[0])
        out_specs.append(out_specs[0])
    return pl.pallas_call(
        functools.partial(solve_kernel, first, edges, again),
        grid=(count,),
        in_specs=in_specs,
        out_specs=out_specs,
        out_shape=out_shape,
        scratch_shapes=[pltpu.VMEM((2, energies, width, width), BF16)],
        compiler_params=pltpu.CompilerParams(vmem_limit_bytes=VMEM),
        cost_estimate=cost(2.5 * count),
        name="solve",
    )(*args)


def grid_spec(energies, width, base=0):
    return pl.BlockSpec((1, 2, energies, width, width), lambda i: (base + i, 0, 0, 0, 0))


def edge_spec(width, base=0):
    return pl.BlockSpec((1, 2, width, width), lambda i: (base + i, 0, 0, 0))


def early_members(blocks, base=0):
    count, _, energies, width, _ = blocks[0].shape
    return list(blocks), [grid_spec(energies, width, base)] * 4


def late_members(blocks, base=0):
    count, _, energies, width, _ = blocks[0].shape
    specs = [grid_spec(energies, width, base)] * 2 + [edge_spec(width, base)] * 4
    return list(blocks), specs


def gate_kernel(*refs):
    pass


def gate(values, after):
    count = len(values)
    return pl.pallas_call(
        gate_kernel,
        in_specs=[ANY] * count + unread(after),
        out_specs=[ANY] * count,
        out_shape=[jax.ShapeDtypeStruct(value.shape, value.dtype) for value in values],
        input_output_aliases={i: i for i in range(count)},
        compiler_params=pltpu.CompilerParams(vmem_limit_bytes=VMEM),
        cost_estimate=cost(2.0),
        name="gate",
    )(*values, *after)


def tiles(width):
    steps = width // TILE

    def run(step_body):
        for part in range(2):

            @pl.loop(0, steps, unroll=UNROLL)
            def _(step):
                step_body(part, pl.ds(pl.multiple_of(step * TILE, TILE), TILE))

    return run


def weighted(terms):
    total = None
    for weight, value in terms:
        term = value if weight is None else weight * value
        total = term if total is None else total + term
    return total


def early_edges_kernel(w_ref, *refs):
    grids, (high_ref, low_ref) = refs[:4], refs[-2:]
    last = grids[0].shape[2] - 1
    width = grids[0].shape[-1]
    above = [w_ref[0, 0, j] for j in range(4)]
    below = [w_ref[0, 2, j] for j in range(4)]

    @tiles(width)
    def _(part, rows):
        high = [(above[j], grids[j][0, part, last, rows, :].astype(F32)) for j in range(4)]
        low = [(below[j], grids[j][0, part, 0, rows, :].astype(F32)) for j in range(4)]
        high_ref[0, part, rows, :] = weighted(high).astype(BF16)
        low_ref[0, part, rows, :] = weighted(low).astype(BF16)


def early_edges(weights, members, after):
    args, specs = early_members(members)
    count, _, energies, width, _ = args[0].shape
    edge = jax.ShapeDtypeStruct((count, 2, width, width), BF16)
    return pl.pallas_call(
        early_edges_kernel,
        grid=(count,),
        in_specs=[pl.BlockSpec(memory_space=pltpu.SMEM)] + specs + unread(after),
        out_specs=[edge_spec(width)] * 2,
        out_shape=[edge, edge],
        compiler_params=pltpu.CompilerParams(vmem_limit_bytes=VMEM),
        cost_estimate=cost(1.7 * count),
        name="early_edges",
    )(weights, *args, *after)


def late_line(refs, part, rows):
    grids, edges = refs[:2], refs[2:]
    lines = []
    for j in range(2):
        line = [edges[2 * j][0, part, rows, :]]
        line += [grids[j][0, part, e, rows, :] for e in range(grids[j].shape[2])]
        line += [edges[2 * j + 1][0, part, rows, :]]
        lines.append([value.astype(F32) for value in line])
    return lines


def late_sum_kernel(pieces, w_ref, *refs):
    members, outs = refs[:6], refs[-pieces:]
    energies, width = members[0].shape[2:4]
    w = [[w_ref[1, o, j] for j in range(2)] for o in range(3)]

    def fill(out_ref):
        @tiles(width)
        def _(part, rows):
            line = late_line(members, part, rows)
            for e in range(energies):
                terms = [(w[o][j], line[j][e + o]) for j in range(2) for o in range(3)]
                out_ref[0, part, e, rows, :] = weighted(terms).astype(BF16)

    if pieces == 1:
        fill(outs[0])
    else:
        for index in range(pieces):
            pl.when(pl.program_id(0) == index)(functools.partial(fill, outs[index]))


def late_sum(weights, members, after, apart=False):
    args, specs = late_members(members)
    count, _, energies, width, _ = args[0].shape
    shape = jax.ShapeDtypeStruct(args[0].shape, BF16)
    out_shape, out_specs = [shape], [grid_spec(energies, width)]
    if apart:
        one = pl.BlockSpec((1, 2, energies, width, width), lambda i: (0, 0, 0, 0, 0))
        out_shape = [jax.ShapeDtypeStruct((1,) + args[0].shape[1:], BF16)] * count
        out_specs = [one] * count
    return pl.pallas_call(
        functools.partial(late_sum_kernel, len(out_shape)),
        grid=(count,),
        in_specs=[pl.BlockSpec(memory_space=pltpu.SMEM)] + specs + unread(after),
        out_specs=out_specs,
        out_shape=out_shape,
        compiler_params=pltpu.CompilerParams(vmem_limit_bytes=VMEM),
        cost_estimate=cost(1.8 * count),
        name="late_sum",
    )(weights, *args, *after)


def finish_kernel(late, charged, w_ref, across_ref, *refs):
    members, received = refs[: 6 if late else 4], refs[6:7] if late else refs[4:6]
    out_ref, down_ref = refs[-3 if charged else -2], refs[-1]
    if charged:
        parts_ref, charge_ref = refs[7 if late else 6], refs[-2]

        @pl.when(pl.program_id(0) == 0)
        def _():
            charge_ref[0] = jnp.sum(parts_ref[...])

    energies, width = members[0].shape[2:4]
    w = [[w_ref[0, o, j] for j in range(4)] for o in range(3)]
    across = across_ref[0]
    lanes = down_ref.shape[1]
    down_ref[...] = jnp.transpose(jnp.broadcast_to(across, (lanes, width)))

    @tiles(width)
    def _(part, rows):
        scale = jnp.concatenate([down_ref[rows, :]] * (width // lanes), axis=1) * across
        if late:
            line = late_line(members, part, rows)
        else:
            line = [
                [None] + [ref[0, part, e, rows, :].astype(F32) for e in range(energies)] + [None]
                for ref in members
            ]
        for e in range(energies):
            terms = [
                (w[o][j], line[j][e + o])
                for j in range(len(line))
                for o in range(3)
                if line[j][e + o] is not None
            ]
            if late:
                terms.append((None, received[0][0, part, e, rows, :].astype(F32)))
            if not late and e == 0:
                terms.append((None, received[0][0, part, rows, :].astype(F32)))
            if not late and e == energies - 1:
                terms.append((None, received[1][0, part, rows, :].astype(F32)))
            out_ref[part, e, 0, rows, :] = (weighted(terms) * scale).astype(BF16)


def finish(sigma, shape, start, weights, across, late, members, received, after, base, parts):
    args, specs = late_members(members, base) if late else early_members(members, base)
    _, _, energies, width, _ = args[0].shape
    count = received[0].shape[0]
    args = [weights, across, *args, *received]
    in_specs = [
        pl.BlockSpec(memory_space=pltpu.SMEM),
        pl.BlockSpec((1, 1, width), lambda i: (start + base + i, 0, 0)),
    ] + specs
    in_specs += [grid_spec(energies, width)] if late else [edge_spec(width)] * 2
    out_shape = [jax.ShapeDtypeStruct(shape, BF16)]
    out_specs = [
        pl.BlockSpec(
            (2, energies, 1, width, width), lambda i: (0, 0, 0, start + base + i, 0)
        )
    ]
    if parts is not None:
        args.append(parts)
        in_specs.append(pl.BlockSpec(parts.shape, lambda i: (0,) * parts.ndim))
        out_shape.append(jax.ShapeDtypeStruct((1,), F32))
        out_specs.append(pl.BlockSpec(memory_space=pltpu.SMEM))
    args += after
    in_specs += unread(after)
    aliases = {}
    if sigma is not None:
        aliases = {len(args): 0}
        args.append(sigma)
        in_specs.append(ANY)
    return pl.pallas_call(
        functools.partial(finish_kernel, late, parts is not None),
        grid=(count,),
        in_specs=in_specs,
        out_specs=out_specs,
        out_shape=out_shape,
        input_output_aliases=aliases,
        scratch_shapes=[pltpu.VMEM((width, 128), F32)],
        compiler_params=pltpu.CompilerParams(vmem_limit_bytes=VMEM),
        cost_estimate=cost(2.2 * count),
        name="finish",
    )(*args)


def range_parts_kernel(count, range_ref, *refs):
    densities, out_ref = refs[:count], refs[-1]
    width = densities[0].shape[-1]
    lanes = lax.broadcasted_iota(jnp.int32, (8, 128), 1)
    pieces = []
    base = 0
    for ref in densities:
        for i in range(ref.shape[0]):
            for half in range(width // 128):
                pieces.append((base, ref[i, :, half * 128 : (half + 1) * 128]))
                base += 128

    def one_range(d, begin):
        end = begin + range_ref[d]
        total = jnp.zeros((8, 128), F32)
        for offset, value in pieces:
            inside = (lanes >= begin - offset) & (lanes < end - offset)
            total = total + jnp.where(inside, value, 0.0)
        out_ref[d] = -jnp.sum(total, axis=0, keepdims=True)
        return end

    lax.fori_loop(0, out_ref.shape[0], one_range, jnp.int32(0))


def range_parts(range_rows, densities, after):
    devices = range_rows.shape[0]
    return pl.pallas_call(
        functools.partial(range_parts_kernel, len(densities)),
        in_specs=[pl.BlockSpec(memory_space=pltpu.SMEM)]
        + [pl.BlockSpec(memory_space=pltpu.VMEM)] * len(densities)
        + unread(after),
        out_specs=pl.BlockSpec(memory_space=pltpu.VMEM),
        out_shape=jax.ShapeDtypeStruct((devices, 1, 128), F32),
        compiler_params=pltpu.CompilerParams(vmem_limit_bytes=VMEM),
        cost_estimate=cost(2.2),
        name="range_parts",
    )(range_rows, *densities, *after)


def own_weights(shifts, emission, absorption):
    me = lax.axis_index("mom")
    folded = []
    for offset in (-1, 0, 1):
        lower = (shifts == -offset).astype(F32)[:, None, None]
        upper = (shifts == offset).astype(F32)[:, None, None]
        folded.append(jnp.sum(lower * emission + upper * absorption, axis=0))
    folded = jnp.stack(folded)
    momenta = jnp.arange(4, dtype=jnp.int32)
    targets = ((me ^ jnp.array([0, 2], jnp.int32))[:, None] == momenta[None]).astype(F32)
    sources = ((me ^ momenta)[:, None] == momenta[None]).astype(F32)
    picked = folded[None, :, None] * targets[:, None, None, :, None] * sources[None, None, :, None, :]
    return jnp.sum(picked, axis=(3, 4))


def body(
    inverse_blocks,
    coupling_blocks,
    shifts,
    emission_weight,
    absorption_weight,
    deform_potential,
    range_rows,
):
    n_energy = lax.axis_size("energy")
    width = inverse_blocks.shape[-1]
    up = [(i, i + 1) for i in range(n_energy - 1)]
    down = [(i + 1, i) for i in range(n_energy - 1)]

    def send(value, axis, pairs, name):
        with jax.named_scope(name):
            return lax.ppermute(value, axis, pairs)

    def core(value, name):
        return send(value, "mom", [(i, i ^ 1) for i in range(4)], name)

    def pair(value, name):
        return send(value, "mom", [(i, i ^ 2) for i in range(4)], name)

    weights = own_weights(shifts, emission_weight, absorption_weight)
    across_scale = deform_potential.reshape(-1, 1, width)

    def run(chunk, previous, after=(), again=False):
        kind, start, count = CHUNKS[chunk]
        return solve(
            inverse_blocks, coupling_blocks, previous, start, count, kind == "late", again, after
        )

    def rise(value, name):
        return send(value, "energy", up, "up" + name)

    def fall(value, name):
        return send(value, "energy", down, "down" + name)

    def done(sigma, chunk, members, got, after=(), base=0, parts=None):
        kind, start, _ = CHUNKS[chunk]
        return finish(
            sigma,
            inverse_blocks.shape,
            start,
            weights,
            across_scale,
            kind == "late",
            members,
            got,
            after,
            base,
            parts,
        )

    g0, n0, low0, high0 = run(0, None)
    up0, c0, beat0 = rise(high0, "0"), core(g0, "core0"), core(n0, "beat0")
    g1, n1 = run(1, g0, (beat0,))
    y1, c1 = pair(g1, "pair1"), core(g1, "core1")
    (low0,) = gate([low0], (g1,))
    down0 = fall(low0, "0")
    g2, n2, low2, high2, h2 = run(2, g1, (c0,), True)
    g3, n3, h3 = run(3, g2, (c1,), True)
    y3 = pair(g3, "pair3")

    low2, high2, h2 = gate([low2, high2, h2], (g3,))
    up2, down2, c2 = rise(high2, "2"), fall(low2, "2"), core(h2, "core2")
    (n0,) = gate([n0], (low2,))

    up0, down0 = gate([up0, down0], (n0, c2))
    core_up0, core_down0 = core(up0, "core_up0"), core(down0, "core_down0")
    (c0,) = gate([c0], (up0,))
    members0 = (g0, c0, up0, down0, core_up0, core_down0)
    (total0,) = late_sum(weights, members0, ())
    x0 = pair(total0, "pair0")

    (y1,) = gate([y1], (total0,))
    core_y1 = core(y1, "core_pair1")
    (c1,) = gate([c1], (y1,))
    members1 = (g1, c1, y1, core_y1)
    high1, low1 = early_edges(weights, members1, ())
    high1, low1, h3 = gate([high1, low1, h3], ())
    up1, down1, c3 = rise(high1, "1"), fall(low1, "1"), core(h3, "core3")
    (n1,) = gate([n1], (low1,))
    (n2,) = gate([n2], (n1, c3))

    up2, down2 = gate([up2, down2], (n2,))
    core_up2, core_down2 = core(up2, "core_up2"), core(down2, "core_down2")
    (c2,) = gate([c2], (up2,))
    members2 = (g2, c2, up2, down2, core_up2, core_down2)
    (total2,) = late_sum(weights, members2, ())
    x2 = pair(total2, "pair2")

    (y3,) = gate([y3], (total2,))
    core_y3 = core(y3, "core_pair3")
    (c3,) = gate([c3], (y3,))
    members3 = (g3, c3, y3, core_y3)
    high3, low3 = early_edges(weights, members3, ())
    up3, down3 = rise(high3, "3"), fall(low3, "3")

    parts = range_parts(range_rows, [n0, n1, n2, n3], (low3,))
    received = lax.all_to_all(parts, ("energy", "mom"), split_axis=0, concat_axis=0, tiled=True)
    (sigma,) = done(None, 0, members0, (x0,), (parts,))
    (sigma,) = done(sigma, 1, members1, (up1, down1))
    (sigma,) = done(sigma, 3, members3, (up3, down3))
    sigma, charge = done(sigma, 2, members2, (x2,), (), 0, received)
    return sigma, charge


def solution(mesh):
    in_specs = (
        P(None, "energy", "mom", None, None),
        P(None, "mom", None, None),
        P(),
        P(),
        P(),
        P(),
        P(),
    )
    out_specs = (P(None, "energy", "mom", None, None), P(("energy", "mom")))
    return jax.shard_map(body, mesh=mesh, in_specs=in_specs, out_specs=out_specs, check_vma=False)
```

```python
import functools

import jax
import jax.numpy as jnp
from jax import lax
from jax.experimental import pallas as pl
from jax.experimental.pallas import tpu as pltpu
from jax.sharding import PartitionSpec as P

CHUNKS = (("late", 0, 2), ("early", 2, 2), ("late", 6, 2), ("early", 4, 2))
VMEM = 63 * 2**20
TILE = 16
UNROLL = 4
ANY = pl.BlockSpec(memory_space=pltpu.HBM)
FACTOR = 100.0


def cost(us):
    return pl.CostEstimate(
        flops=int(us * FACTOR * 1.15e9), bytes_accessed=0, transcendentals=0
    )


F32 = jnp.float32
BF16 = jnp.bfloat16


def unread(values):
    return [ANY] * len(values)


def dot(left, right, transpose=False):
    dims = (((1,), (1 if transpose else 0,)), ((), ()))
    return lax.dot_general(left, right, dims, preferred_element_type=F32)


def complex_dot(left, right):
    wide = jnp.concatenate(left, axis=1)
    re = dot(wide, jnp.concatenate([right[0], -right[1]], axis=0))
    im = dot(wide, jnp.concatenate([right[1], right[0]], axis=0))
    return re.astype(BF16), im.astype(BF16)


def complex_dot_adjoint(left, right):
    wide = jnp.concatenate(left, axis=1)
    re = dot(wide, jnp.concatenate([right[0], right[1]], axis=1), True)
    im = dot(wide, jnp.concatenate([-right[1], right[0]], axis=1), True)
    return re.astype(BF16), im.astype(BF16)


def solve_kernel(first, edges, again, *refs):
    refs = list(refs)
    a_ref, t_ref = refs[:2]
    previous_ref = None if first else refs[2]
    carry = refs.pop()
    again_ref = refs.pop() if again else None
    low_ref, high_ref = refs[-2:] if edges else (None, None)
    outs = refs[:-2] if edges else refs
    green_ref, density_ref = outs[-2:]
    energies = a_ref.shape[1]
    width = a_ref.shape[-1]
    t = (t_ref[0, 0], t_ref[1, 0])
    if not first:

        @pl.when(pl.program_id(0) == 0)
        def _():
            carry[...] = previous_ref[0]

    rows = lax.broadcasted_iota(jnp.int32, (width, width), 0)
    columns = lax.broadcasted_iota(jnp.int32, (width, width), 1)
    total = jnp.zeros((8, width), F32)
    if first:

        @pl.when(pl.program_id(0) == 0)
        def _():
            couple = complex_dot_adjoint(t, t)
            for e in range(energies):
                carry[0, e], carry[1, e] = couple

        @pl.when(pl.program_id(0) > 0)
        def _():
            for e in range(energies):
                left = complex_dot(t, (carry[0, e], carry[1, e]))
                carry[0, e], carry[1, e] = complex_dot_adjoint(left, t)

    blocks = [(a_ref[0, e, 0], a_ref[1, e, 0]) for e in range(energies)]
    couples = [(carry[0, e], carry[1, e]) for e in range(energies)]
    if not first:
        lefts = [complex_dot(t, green) for green in couples]
        couples = [complex_dot_adjoint(left, t) for left in lefts]
    inners = [complex_dot(a, couple) for a, couple in zip(blocks, couples)]
    for e in range(energies):
        a, inner = blocks[e], inners[e]
        wide = jnp.concatenate(inner, axis=1)
        re = a[0].astype(F32) + dot(wide, jnp.concatenate([a[0], -a[1]], axis=0))
        im = a[1].astype(F32) + dot(wide, jnp.concatenate([a[1], a[0]], axis=0))
        re, im = re.astype(BF16), im.astype(BF16)
        carry[0, e] = re
        carry[1, e] = im
        green_ref[0, 0, e] = re
        green_ref[0, 1, e] = im
        if again:
            again_ref[0, 0, e] = re
            again_ref[0, 1, e] = im
        if edges and e == 0:
            low_ref[0, 0] = re
            low_ref[0, 1] = im
        if edges and e == energies - 1:
            high_ref[0, 0] = re
            high_ref[0, 1] = im
        diagonal = jnp.where(rows == columns, im.astype(F32), 0.0)
        total = total + jnp.sum(diagonal.reshape(width // 8, 8, width), axis=0)
    density_ref[0] = total


def solve(inverse, coupled, previous, start, count, edges, again, after=()):
    _, energies, _, total_rows, width = inverse.shape
    first = previous is None
    args = [inverse, coupled]
    in_specs = [
        pl.BlockSpec((2, energies, 1, width, width), lambda i: (0, 0, 0, start + i, 0)),
        pl.BlockSpec((2, 1, width, width), lambda i: (0, 0, start + i, 0)),
    ]
    if not first:
        last = previous.shape[0] - 1
        args.append(previous)
        in_specs.append(
            pl.BlockSpec((1, 2, energies, width, width), lambda i: (last, 0, 0, 0, 0))
        )
    args.extend(after)
    in_specs.extend(unread(after))
    out_shape = [
        jax.ShapeDtypeStruct((count, 2, energies, width, width), BF16),
        jax.ShapeDtypeStruct((count, 8, width), F32),
    ]
    out_specs = [
        pl.BlockSpec((1, 2, energies, width, width), lambda i: (i, 0, 0, 0, 0)),
        pl.BlockSpec((1, 8, width), lambda i: (i, 0, 0)),
    ]
    if edges:
        for _ in range(2):
            out_shape.append(jax.ShapeDtypeStruct((count, 2, width, width), BF16))
            out_specs.append(pl.BlockSpec((1, 2, width, width), lambda i: (i, 0, 0, 0)))
    if again:
        out_shape.append(out_shape[0])
        out_specs.append(out_specs[0])
    return pl.pallas_call(
        functools.partial(solve_kernel, first, edges, again),
        grid=(count,),
        in_specs=in_specs,
        out_specs=out_specs,
        out_shape=out_shape,
        scratch_shapes=[pltpu.VMEM((2, energies, width, width), BF16)],
        compiler_params=pltpu.CompilerParams(vmem_limit_bytes=VMEM),
        cost_estimate=cost(2.5 * count),
        name="solve",
    )(*args)


def grid_spec(energies, width):
    return pl.BlockSpec((1, 2, energies, width, width), lambda i: (i, 0, 0, 0, 0))


def edge_spec(width):
    return pl.BlockSpec((1, 2, width, width), lambda i: (i, 0, 0, 0))


def gate_kernel(*refs):
    pass


def gate(values, after):
    count = len(values)
    return pl.pallas_call(
        gate_kernel,
        in_specs=[ANY] * count + unread(after),
        out_specs=[ANY] * count,
        out_shape=[jax.ShapeDtypeStruct(value.shape, value.dtype) for value in values],
        input_output_aliases={i: i for i in range(count)},
        compiler_params=pltpu.CompilerParams(vmem_limit_bytes=VMEM),
        cost_estimate=cost(2.0),
        name="gate",
    )(*values, *after)


def tiles(width):
    steps = width // TILE

    def run(step_body):
        for part in range(2):

            @pl.loop(0, steps, unroll=UNROLL)
            def _(step):
                step_body(part, pl.ds(pl.multiple_of(step * TILE, TILE), TILE))

    return run


def weighted(terms):
    total = None
    for weight, value in terms:
        term = value if weight is None else weight * value
        total = term if total is None else total + term
    return total


def early_edges_kernel(w_ref, *refs):
    grids, (high_ref, low_ref, local_ref) = refs[:4], refs[-3:]
    energies, width = grids[0].shape[2:4]
    w = [[w_ref[0, o, j] for j in range(4)] for o in range(3)]

    @tiles(width)
    def _(part, rows):
        line = [
            [ref[0, part, e, rows, :].astype(F32) for e in range(energies)] for ref in grids
        ]
        high = [(w[0][j], line[j][energies - 1]) for j in range(4)]
        low = [(w[2][j], line[j][0]) for j in range(4)]
        high_ref[0, part, rows, :] = weighted(high).astype(BF16)
        low_ref[0, part, rows, :] = weighted(low).astype(BF16)
        for e in range(energies):
            terms = [
                (w[o][j], line[j][e + o - 1])
                for j in range(4)
                for o in range(3)
                if 0 <= e + o - 1 < energies
            ]
            local_ref[0, part, e, rows, :] = weighted(terms).astype(BF16)


def early_edges(weights, members, after):
    count, _, energies, width, _ = members[0].shape
    edge = jax.ShapeDtypeStruct((count, 2, width, width), BF16)
    spec = grid_spec(energies, width)
    return pl.pallas_call(
        early_edges_kernel,
        grid=(count,),
        in_specs=[pl.BlockSpec(memory_space=pltpu.SMEM)] + [spec] * 4 + unread(after),
        out_specs=[edge_spec(width)] * 2 + [spec],
        out_shape=[edge, edge, jax.ShapeDtypeStruct(members[0].shape, BF16)],
        compiler_params=pltpu.CompilerParams(vmem_limit_bytes=VMEM),
        cost_estimate=cost(1.7 * count),
        name="early_edges",
    )(weights, *members, *after)


def late_line(refs, part, rows):
    grids, edges = refs[:2], refs[2:]
    lines = []
    for j in range(2):
        line = [edges[2 * j][0, part, rows, :]]
        line += [grids[j][0, part, e, rows, :] for e in range(grids[j].shape[2])]
        line += [edges[2 * j + 1][0, part, rows, :]]
        lines.append([value.astype(F32) for value in line])
    return lines


def late_sum_kernel(w_ref, *refs):
    members, outs = refs[:6], refs[-2:]
    energies, width = members[0].shape[2:4]
    w = [[[w_ref[t, o, j] for j in range(2)] for o in range(3)] for t in range(2)]

    @tiles(width)
    def _(part, rows):
        line = late_line(members, part, rows)
        for target, out_ref in zip((1, 0), outs):
            for e in range(energies):
                terms = [(w[target][o][j], line[j][e + o]) for j in range(2) for o in range(3)]
                out_ref[0, part, e, rows, :] = weighted(terms).astype(BF16)


def late_sum(weights, members, after):
    count, _, energies, width, _ = members[0].shape
    spec = grid_spec(energies, width)
    return pl.pallas_call(
        late_sum_kernel,
        grid=(count,),
        in_specs=[pl.BlockSpec(memory_space=pltpu.SMEM)]
        + [spec] * 2
        + [edge_spec(width)] * 4
        + unread(after),
        out_specs=[spec, spec],
        out_shape=[jax.ShapeDtypeStruct(members[0].shape, BF16)] * 2,
        compiler_params=pltpu.CompilerParams(vmem_limit_bytes=VMEM),
        cost_estimate=cost(1.8 * count),
        name="late_sum",
    )(weights, *members, *after)


def finish_kernel(late, charged, across_ref, local_ref, *refs):
    received = refs[:1] if late else refs[:2]
    out_ref, down_ref = refs[-3 if charged else -2], refs[-1]
    if charged:
        parts_ref, charge_ref = refs[len(received)], refs[-2]

        @pl.when(pl.program_id(0) == 0)
        def _():
            charge_ref[0] = jnp.sum(parts_ref[...])

    energies, width = local_ref.shape[2:4]
    across = across_ref[0]
    lanes = down_ref.shape[1]
    down_ref[...] = jnp.transpose(jnp.broadcast_to(across, (lanes, width)))

    @tiles(width)
    def _(part, rows):
        scale = jnp.concatenate([down_ref[rows, :]] * (width // lanes), axis=1) * across
        for e in range(energies):
            total = local_ref[0, part, e, rows, :].astype(F32)
            if late:
                total = total + received[0][0, part, e, rows, :].astype(F32)
            if not late and e == 0:
                total = total + received[0][0, part, rows, :].astype(F32)
            if not late and e == energies - 1:
                total = total + received[1][0, part, rows, :].astype(F32)
            out_ref[part, e, 0, rows, :] = (total * scale).astype(BF16)


def finish(sigma, shape, start, across, late, local, received, after, parts):
    count, _, energies, width, _ = local.shape
    args = [across, local, *received]
    in_specs = [
        pl.BlockSpec((1, 1, width), lambda i: (start + i, 0, 0)),
        grid_spec(energies, width),
    ]
    in_specs += [grid_spec(energies, width)] if late else [edge_spec(width)] * 2
    out_shape = [jax.ShapeDtypeStruct(shape, BF16)]
    out_specs = [
        pl.BlockSpec((2, energies, 1, width, width), lambda i: (0, 0, 0, start + i, 0))
    ]
    if parts is not None:
        args.append(parts)
        in_specs.append(pl.BlockSpec(parts.shape, lambda i: (0,) * parts.ndim))
        out_shape.append(jax.ShapeDtypeStruct((1,), F32))
        out_specs.append(pl.BlockSpec(memory_space=pltpu.SMEM))
    args += after
    in_specs += unread(after)
    aliases = {}
    if sigma is not None:
        aliases = {len(args): 0}
        args.append(sigma)
        in_specs.append(ANY)
    return pl.pallas_call(
        functools.partial(finish_kernel, late, parts is not None),
        grid=(count,),
        in_specs=in_specs,
        out_specs=out_specs,
        out_shape=out_shape,
        input_output_aliases=aliases,
        scratch_shapes=[pltpu.VMEM((width, 128), F32)],
        compiler_params=pltpu.CompilerParams(vmem_limit_bytes=VMEM),
        cost_estimate=cost(2.2 * count),
        name="finish",
    )(*args)


def range_parts_kernel(count, range_ref, *refs):
    densities, out_ref = refs[:count], refs[-1]
    width = densities[0].shape[-1]
    lanes = lax.broadcasted_iota(jnp.int32, (8, 128), 1)
    pieces = []
    base = 0
    for ref in densities:
        for i in range(ref.shape[0]):
            for half in range(width // 128):
                pieces.append((base, ref[i, :, half * 128 : (half + 1) * 128]))
                base += 128

    def one_range(d, begin):
        end = begin + range_ref[d]
        total = jnp.zeros((8, 128), F32)
        for offset, value in pieces:
            inside = (lanes >= begin - offset) & (lanes < end - offset)
            total = total + jnp.where(inside, value, 0.0)
        out_ref[d] = -jnp.sum(total, axis=0, keepdims=True)
        return end

    lax.fori_loop(0, out_ref.shape[0], one_range, jnp.int32(0), unroll=4)


def range_parts(range_rows, densities, after):
    devices = range_rows.shape[0]
    return pl.pallas_call(
        functools.partial(range_parts_kernel, len(densities)),
        in_specs=[pl.BlockSpec(memory_space=pltpu.SMEM)]
        + [pl.BlockSpec(memory_space=pltpu.VMEM)] * len(densities)
        + unread(after),
        out_specs=pl.BlockSpec(memory_space=pltpu.VMEM),
        out_shape=jax.ShapeDtypeStruct((devices, 1, 128), F32),
        compiler_params=pltpu.CompilerParams(vmem_limit_bytes=VMEM),
        cost_estimate=cost(2.2),
        name="range_parts",
    )(range_rows, *densities, *after)


def own_weights_kernel(shift_ref, emission_ref, absorption_ref, *refs):
    out_ref = refs[-1]
    me = lax.axis_index("mom")
    zero = jnp.float32(0)
    for target in range(2):
        for offset in (-1, 0, 1):
            for j in range(4):
                total = zero
                for p in range(shift_ref.shape[0]):
                    emitted = emission_ref[p, me ^ (2 * target), me ^ j]
                    absorbed = absorption_ref[p, me ^ (2 * target), me ^ j]
                    total = total + jnp.where(shift_ref[p] == -offset, emitted, zero)
                    total = total + jnp.where(shift_ref[p] == offset, absorbed, zero)
                out_ref[target, offset + 1, j] = total


def own_weights(shifts, emission, absorption, after):
    smem = pl.BlockSpec(memory_space=pltpu.SMEM)
    return pl.pallas_call(
        own_weights_kernel,
        in_specs=[smem] * 3 + unread(after),
        out_specs=smem,
        out_shape=jax.ShapeDtypeStruct((2, 3, 4), F32),
        compiler_params=pltpu.CompilerParams(vmem_limit_bytes=VMEM),
        cost_estimate=cost(0.5),
        name="own_weights",
    )(shifts, emission, absorption, *after)


def body(
    inverse_blocks,
    coupling_blocks,
    shifts,
    emission_weight,
    absorption_weight,
    deform_potential,
    range_rows,
):
    n_energy = lax.axis_size("energy")
    width = inverse_blocks.shape[-1]
    up = [(i, i + 1) for i in range(n_energy - 1)]
    down = [(i + 1, i) for i in range(n_energy - 1)]

    def send(value, axis, pairs, name):
        with jax.named_scope(name):
            return lax.ppermute(value, axis, pairs)

    def core(value, name):
        return send(value, "mom", [(i, i ^ 1) for i in range(4)], name)

    def pair(value, name):
        return send(value, "mom", [(i, i ^ 2) for i in range(4)], name)

    across_scale = deform_potential.reshape(-1, 1, width)

    def run(chunk, previous, after=(), again=False):
        kind, start, count = CHUNKS[chunk]
        return solve(
            inverse_blocks, coupling_blocks, previous, start, count, kind == "late", again, after
        )

    def rise(value, name):
        return send(value, "energy", up, "up" + name)

    def fall(value, name):
        return send(value, "energy", down, "down" + name)

    def done(sigma, chunk, local, got, after=(), parts=None):
        kind, start, _ = CHUNKS[chunk]
        return finish(
            sigma,
            inverse_blocks.shape,
            start,
            across_scale,
            kind == "late",
            local,
            got,
            after,
            parts,
        )

    g0, n0, low0, high0 = run(0, None)
    up0, c0 = rise(high0, "0"), core(g0, "core0")
    g1, n1 = run(1, g0, (c0,))
    y1, c1 = pair(g1, "pair1"), core(g1, "core1")
    (low0,) = gate([low0], (g1,))
    down0 = fall(low0, "0")
    g3, n3, h3 = run(3, g1, (c1,), True)
    y3 = pair(g3, "pair3")
    g2, n2, low2, high2, h2 = run(2, g3, (), True)
    weights = own_weights(shifts, emission_weight, absorption_weight, (n2,))

    low2, high2, h2 = gate([low2, high2, h2], (weights,))
    up2, down2, c2 = rise(high2, "2"), fall(low2, "2"), core(h2, "core2")
    (n0,) = gate([n0], (low2,))

    up0, down0 = gate([up0, down0], (n0, c2))
    core_up0, core_down0 = core(up0, "core_up0"), core(down0, "core_down0")
    (c0,) = gate([c0], (up0,))
    members0 = (g0, c0, up0, down0, core_up0, core_down0)
    total0, local0 = late_sum(weights, members0, ())
    x0 = pair(total0, "pair0")
    y1, h3 = gate([y1, h3], (total0,))
    core_y1, c3 = core(y1, "core_pair1"), core(h3, "core3")
    (c1,) = gate([c1], (y1,))

    members1 = (g1, c1, y1, core_y1)
    high1, low1, local1 = early_edges(weights, members1, (c3,))
    high1, low1, n1 = gate([high1, low1, n1], ())
    up1, down1, beat1 = rise(high1, "1"), fall(low1, "1"), core(n1, "beat1")
    (n2,) = gate([n2], (n1,))
    (n3,) = gate([n3], (n2, beat1))

    up2, down2 = gate([up2, down2], (n3,))
    core_up2, core_down2 = core(up2, "core_up2"), core(down2, "core_down2")
    (c2,) = gate([c2], (up2,))
    (y3,) = gate([y3], (c2, core_up2, core_down2))
    core_y3 = core(y3, "core_pair3")
    members2 = (g2, c2, up2, down2, core_up2, core_down2)
    total2, local2 = late_sum(weights, members2, (y3,))
    x2 = pair(total2, "pair2")

    members3 = (g3, c3, y3, core_y3)
    high3, low3, local3 = early_edges(weights, members3, (total2,))
    up3, down3 = rise(high3, "3"), fall(low3, "3")

    parts = range_parts(range_rows, [n0, n1, n3, n2], (low3,))
    received = lax.all_to_all(parts, ("energy", "mom"), split_axis=0, concat_axis=0, tiled=True)
    (sigma,) = done(None, 0, local0, (x0,), (parts,))
    (sigma,) = done(sigma, 1, local1, (up1, down1))
    (sigma,) = done(sigma, 3, local3, (up3, down3))
    sigma, charge = done(sigma, 2, local2, (x2,), (), received)
    return sigma, charge


def solution(mesh):
    in_specs = (
        P(None, "energy", "mom", None, None),
        P(None, "mom", None, None),
        P(),
        P(),
        P(),
        P(),
        P(),
    )
    out_specs = (P(None, "energy", "mom", None, None), P(("energy", "mom")))
    return jax.shard_map(body, mesh=mesh, in_specs=in_specs, out_specs=out_specs, check_vma=False)
```

```python
import functools

import jax
import jax.numpy as jnp
from jax import lax
from jax.experimental import pallas as pl
from jax.experimental.pallas import tpu as pltpu
from jax.sharding import PartitionSpec as P

CHUNKS = (("late", 0, 2), ("early", 2, 2), ("late", 6, 2), ("early", 4, 2))
VMEM = 63 * 2**20
TILE = 16
UNROLL = 16
ANY = pl.BlockSpec(memory_space=pltpu.HBM)
FACTOR = 100.0


def cost(us):
    return pl.CostEstimate(
        flops=int(us * FACTOR * 1.15e9), bytes_accessed=0, transcendentals=0
    )


F32 = jnp.float32
BF16 = jnp.bfloat16


def unread(values):
    return [ANY] * len(values)


def dot(left, right, transpose=False):
    dims = (((1,), (1 if transpose else 0,)), ((), ()))
    return lax.dot_general(left, right, dims, preferred_element_type=F32)


def complex_dot(left, right):
    wide = jnp.concatenate(left, axis=1)
    re = dot(wide, jnp.concatenate([right[0], -right[1]], axis=0))
    im = dot(wide, jnp.concatenate([right[1], right[0]], axis=0))
    return re.astype(BF16), im.astype(BF16)


def complex_dot_adjoint(left, right):
    wide = jnp.concatenate(left, axis=1)
    re = dot(wide, jnp.concatenate([right[0], right[1]], axis=1), True)
    im = dot(wide, jnp.concatenate([-right[1], right[0]], axis=1), True)
    return re.astype(BF16), im.astype(BF16)


def solve_kernel(first, edges, again, *refs):
    refs = list(refs)
    a_ref, t_ref = refs[:2]
    previous_ref = None if first else refs[2]
    carry = refs.pop()
    again_ref = refs.pop() if again else None
    low_ref, high_ref = refs[-2:] if edges else (None, None)
    outs = refs[:-2] if edges else refs
    green_ref, density_ref = outs[-2:]
    energies = a_ref.shape[1]
    width = a_ref.shape[-1]
    t = (t_ref[0, 0], t_ref[1, 0])
    if not first:

        @pl.when(pl.program_id(0) == 0)
        def _():
            carry[...] = previous_ref[0]

    rows = lax.broadcasted_iota(jnp.int32, (width, width), 0)
    columns = lax.broadcasted_iota(jnp.int32, (width, width), 1)
    total = jnp.zeros((8, width), F32)
    if first:

        @pl.when(pl.program_id(0) == 0)
        def _():
            couple = complex_dot_adjoint(t, t)
            for e in range(energies):
                carry[0, e], carry[1, e] = couple

        @pl.when(pl.program_id(0) > 0)
        def _():
            for e in range(energies):
                left = complex_dot(t, (carry[0, e], carry[1, e]))
                carry[0, e], carry[1, e] = complex_dot_adjoint(left, t)

    blocks = [(a_ref[0, e, 0], a_ref[1, e, 0]) for e in range(energies)]
    couples = [(carry[0, e], carry[1, e]) for e in range(energies)]
    if not first:
        lefts = [complex_dot(t, green) for green in couples]
        couples = [complex_dot_adjoint(left, t) for left in lefts]
    inners = [complex_dot(a, couple) for a, couple in zip(blocks, couples)]
    for e in range(energies):
        a, inner = blocks[e], inners[e]
        wide = jnp.concatenate(inner, axis=1)
        re = a[0].astype(F32) + dot(wide, jnp.concatenate([a[0], -a[1]], axis=0))
        im = a[1].astype(F32) + dot(wide, jnp.concatenate([a[1], a[0]], axis=0))
        re, im = re.astype(BF16), im.astype(BF16)
        carry[0, e] = re
        carry[1, e] = im
        green_ref[0, 0, e] = re
        green_ref[0, 1, e] = im
        if again:
            again_ref[0, 0, e] = re
            again_ref[0, 1, e] = im
        if edges and e == 0:
            low_ref[0, 0] = re
            low_ref[0, 1] = im
        if edges and e == energies - 1:
            high_ref[0, 0] = re
            high_ref[0, 1] = im
        diagonal = jnp.where(rows == columns, im.astype(F32), 0.0)
        total = total + jnp.sum(diagonal.reshape(width // 8, 8, width), axis=0)
    density_ref[0] = total


def solve(inverse, coupled, previous, start, count, edges, again, after=()):
    _, energies, _, total_rows, width = inverse.shape
    first = previous is None
    args = [inverse, coupled]
    in_specs = [
        pl.BlockSpec((2, energies, 1, width, width), lambda i: (0, 0, 0, start + i, 0)),
        pl.BlockSpec((2, 1, width, width), lambda i: (0, 0, start + i, 0)),
    ]
    if not first:
        last = previous.shape[0] - 1
        args.append(previous)
        in_specs.append(
            pl.BlockSpec((1, 2, energies, width, width), lambda i: (last, 0, 0, 0, 0))
        )
    args.extend(after)
    in_specs.extend(unread(after))
    out_shape = [
        jax.ShapeDtypeStruct((count, 2, energies, width, width), BF16),
        jax.ShapeDtypeStruct((count, 8, width), F32),
    ]
    out_specs = [
        pl.BlockSpec((1, 2, energies, width, width), lambda i: (i, 0, 0, 0, 0)),
        pl.BlockSpec((1, 8, width), lambda i: (i, 0, 0)),
    ]
    if edges:
        for _ in range(2):
            out_shape.append(jax.ShapeDtypeStruct((count, 2, width, width), BF16))
            out_specs.append(pl.BlockSpec((1, 2, width, width), lambda i: (i, 0, 0, 0)))
    if again:
        out_shape.append(out_shape[0])
        out_specs.append(out_specs[0])
    return pl.pallas_call(
        functools.partial(solve_kernel, first, edges, again),
        grid=(count,),
        in_specs=in_specs,
        out_specs=out_specs,
        out_shape=out_shape,
        scratch_shapes=[pltpu.VMEM((2, energies, width, width), BF16)],
        compiler_params=pltpu.CompilerParams(vmem_limit_bytes=VMEM),
        cost_estimate=cost(2.5 * count),
        name="solve",
    )(*args)


def grid_spec(energies, width):
    return pl.BlockSpec((1, 2, energies, width, width), lambda i: (i, 0, 0, 0, 0))


def edge_spec(width):
    return pl.BlockSpec((1, 2, width, width), lambda i: (i, 0, 0, 0))


def gate_kernel(*refs):
    pass


def gate(values, after):
    count = len(values)
    return pl.pallas_call(
        gate_kernel,
        in_specs=[ANY] * count + unread(after),
        out_specs=[ANY] * count,
        out_shape=[jax.ShapeDtypeStruct(value.shape, value.dtype) for value in values],
        input_output_aliases={i: i for i in range(count)},
        compiler_params=pltpu.CompilerParams(vmem_limit_bytes=VMEM),
        cost_estimate=cost(2.0),
        name="gate",
    )(*values, *after)


def tiles(width):
    steps = width // TILE

    def run(step_body):
        for part in range(2):

            @pl.loop(0, steps, unroll=UNROLL)
            def _(step):
                step_body(part, pl.ds(pl.multiple_of(step * TILE, TILE), TILE))

    return run


def weighted(terms):
    total = None
    for weight, value in terms:
        term = value if weight is None else weight * value
        total = term if total is None else total + term
    return total


def early_edges_kernel(w_ref, *refs):
    grids, (high_ref, low_ref, local_ref) = refs[:4], refs[-3:]
    energies, width = grids[0].shape[2:4]
    w = [[w_ref[0, o, j] for j in range(4)] for o in range(3)]

    @tiles(width)
    def _(part, rows):
        line = [
            [ref[0, part, e, rows, :].astype(F32) for e in range(energies)] for ref in grids
        ]
        high = [(w[0][j], line[j][energies - 1]) for j in range(4)]
        low = [(w[2][j], line[j][0]) for j in range(4)]
        high_ref[0, part, rows, :] = weighted(high).astype(BF16)
        low_ref[0, part, rows, :] = weighted(low).astype(BF16)
        for e in range(energies):
            terms = [
                (w[o][j], line[j][e + o - 1])
                for j in range(4)
                for o in range(3)
                if 0 <= e + o - 1 < energies
            ]
            local_ref[0, part, e, rows, :] = weighted(terms).astype(BF16)


def early_edges(weights, members, after):
    count, _, energies, width, _ = members[0].shape
    edge = jax.ShapeDtypeStruct((count, 2, width, width), BF16)
    spec = grid_spec(energies, width)
    return pl.pallas_call(
        early_edges_kernel,
        grid=(count,),
        in_specs=[pl.BlockSpec(memory_space=pltpu.SMEM)] + [spec] * 4 + unread(after),
        out_specs=[edge_spec(width)] * 2 + [spec],
        out_shape=[edge, edge, jax.ShapeDtypeStruct(members[0].shape, BF16)],
        compiler_params=pltpu.CompilerParams(vmem_limit_bytes=VMEM),
        cost_estimate=cost(1.7 * count),
        name="early_edges",
    )(weights, *members, *after)


def late_line(refs, part, rows):
    grids, edges = refs[:2], refs[2:]
    lines = []
    for j in range(2):
        line = [edges[2 * j][0, part, rows, :]]
        line += [grids[j][0, part, e, rows, :] for e in range(grids[j].shape[2])]
        line += [edges[2 * j + 1][0, part, rows, :]]
        lines.append([value.astype(F32) for value in line])
    return lines


def late_sum_kernel(w_ref, *refs):
    members, outs = refs[:6], refs[-2:]
    energies, width = members[0].shape[2:4]
    w = [[[w_ref[t, o, j] for j in range(2)] for o in range(3)] for t in range(2)]

    @tiles(width)
    def _(part, rows):
        line = late_line(members, part, rows)
        for target, out_ref in zip((1, 0), outs):
            for e in range(energies):
                terms = [(w[target][o][j], line[j][e + o]) for j in range(2) for o in range(3)]
                out_ref[0, part, e, rows, :] = weighted(terms).astype(BF16)


def late_sum(weights, members, after):
    count, _, energies, width, _ = members[0].shape
    spec = grid_spec(energies, width)
    return pl.pallas_call(
        late_sum_kernel,
        grid=(count,),
        in_specs=[pl.BlockSpec(memory_space=pltpu.SMEM)]
        + [spec] * 2
        + [edge_spec(width)] * 4
        + unread(after),
        out_specs=[spec, spec],
        out_shape=[jax.ShapeDtypeStruct(members[0].shape, BF16)] * 2,
        compiler_params=pltpu.CompilerParams(vmem_limit_bytes=VMEM),
        cost_estimate=cost(1.8 * count),
        name="late_sum",
    )(weights, *members, *after)


def finish_kernel(late, charged, across_ref, local_ref, *refs):
    received = refs[:1] if late else refs[:2]
    out_ref, down_ref = refs[-3 if charged else -2], refs[-1]
    if charged:
        parts_ref, charge_ref = refs[len(received)], refs[-2]

        @pl.when(pl.program_id(0) == 0)
        def _():
            charge_ref[0] = jnp.sum(parts_ref[...])

    energies, width = local_ref.shape[2:4]
    across = across_ref[0]
    lanes = down_ref.shape[1]
    down_ref[...] = jnp.transpose(jnp.broadcast_to(across, (lanes, width)))

    @tiles(width)
    def _(part, rows):
        scale = jnp.concatenate([down_ref[rows, :]] * (width // lanes), axis=1) * across
        for e in range(energies):
            total = local_ref[0, part, e, rows, :].astype(F32)
            if late:
                total = total + received[0][0, part, e, rows, :].astype(F32)
            if not late and e == 0:
                total = total + received[0][0, part, rows, :].astype(F32)
            if not late and e == energies - 1:
                total = total + received[1][0, part, rows, :].astype(F32)
            out_ref[part, e, 0, rows, :] = (total * scale).astype(BF16)


def finish(sigma, shape, start, across, late, local, received, after, parts):
    count, _, energies, width, _ = local.shape
    args = [across, local, *received]
    in_specs = [
        pl.BlockSpec((1, 1, width), lambda i: (start + i, 0, 0)),
        grid_spec(energies, width),
    ]
    in_specs += [grid_spec(energies, width)] if late else [edge_spec(width)] * 2
    out_shape = [jax.ShapeDtypeStruct(shape, BF16)]
    out_specs = [
        pl.BlockSpec((2, energies, 1, width, width), lambda i: (0, 0, 0, start + i, 0))
    ]
    if parts is not None:
        args.append(parts)
        in_specs.append(pl.BlockSpec(parts.shape, lambda i: (0,) * parts.ndim))
        out_shape.append(jax.ShapeDtypeStruct((1,), F32))
        out_specs.append(pl.BlockSpec(memory_space=pltpu.SMEM))
    args += after
    in_specs += unread(after)
    aliases = {}
    if sigma is not None:
        aliases = {len(args): 0}
        args.append(sigma)
        in_specs.append(ANY)
    return pl.pallas_call(
        functools.partial(finish_kernel, late, parts is not None),
        grid=(count,),
        in_specs=in_specs,
        out_specs=out_specs,
        out_shape=out_shape,
        input_output_aliases=aliases,
        scratch_shapes=[pltpu.VMEM((width, 128), F32)],
        compiler_params=pltpu.CompilerParams(vmem_limit_bytes=VMEM),
        cost_estimate=cost(2.2 * count),
        name="finish",
    )(*args)


def range_parts_kernel(count, range_ref, *refs):
    densities, out_ref = refs[:count], refs[-1]
    width = densities[0].shape[-1]
    lanes = lax.broadcasted_iota(jnp.int32, (8, 128), 1)
    pieces = []
    base = 0
    for ref in densities:
        for i in range(ref.shape[0]):
            for half in range(width // 128):
                pieces.append((base, ref[i, :, half * 128 : (half + 1) * 128]))
                base += 128

    def one_range(d, begin):
        end = begin + range_ref[d]
        total = jnp.zeros((8, 128), F32)
        for offset, value in pieces:
            inside = (lanes >= begin - offset) & (lanes < end - offset)
            total = total + jnp.where(inside, value, 0.0)
        out_ref[d] = -jnp.sum(total, axis=0, keepdims=True)
        return end

    lax.fori_loop(0, out_ref.shape[0], one_range, jnp.int32(0), unroll=4)


def range_parts(range_rows, densities, after):
    devices = range_rows.shape[0]
    return pl.pallas_call(
        functools.partial(range_parts_kernel, len(densities)),
        in_specs=[pl.BlockSpec(memory_space=pltpu.SMEM)]
        + [pl.BlockSpec(memory_space=pltpu.VMEM)] * len(densities)
        + unread(after),
        out_specs=pl.BlockSpec(memory_space=pltpu.VMEM),
        out_shape=jax.ShapeDtypeStruct((devices, 1, 128), F32),
        compiler_params=pltpu.CompilerParams(vmem_limit_bytes=VMEM),
        cost_estimate=cost(2.2),
        name="range_parts",
    )(range_rows, *densities, *after)


def own_weights_kernel(shift_ref, emission_ref, absorption_ref, *refs):
    out_ref = refs[-1]
    me = lax.axis_index("mom")
    zero = jnp.float32(0)
    for target in range(2):
        for offset in (-1, 0, 1):
            for j in range(4):
                total = zero
                for p in range(shift_ref.shape[0]):
                    emitted = emission_ref[p, me ^ (2 * target), me ^ j]
                    absorbed = absorption_ref[p, me ^ (2 * target), me ^ j]
                    total = total + jnp.where(shift_ref[p] == -offset, emitted, zero)
                    total = total + jnp.where(shift_ref[p] == offset, absorbed, zero)
                out_ref[target, offset + 1, j] = total


def own_weights(shifts, emission, absorption, after):
    smem = pl.BlockSpec(memory_space=pltpu.SMEM)
    return pl.pallas_call(
        own_weights_kernel,
        in_specs=[smem] * 3 + unread(after),
        out_specs=smem,
        out_shape=jax.ShapeDtypeStruct((2, 3, 4), F32),
        compiler_params=pltpu.CompilerParams(vmem_limit_bytes=VMEM),
        cost_estimate=cost(0.5),
        name="own_weights",
    )(shifts, emission, absorption, *after)


def body(
    inverse_blocks,
    coupling_blocks,
    shifts,
    emission_weight,
    absorption_weight,
    deform_potential,
    range_rows,
):
    n_energy = lax.axis_size("energy")
    width = inverse_blocks.shape[-1]
    up = [(i, i + 1) for i in range(n_energy - 1)]
    down = [(i + 1, i) for i in range(n_energy - 1)]

    def send(value, axis, pairs, name):
        with jax.named_scope(name):
            return lax.ppermute(value, axis, pairs)

    def core(value, name):
        return send(value, "mom", [(i, i ^ 1) for i in range(4)], name)

    def pair(value, name):
        return send(value, "mom", [(i, i ^ 2) for i in range(4)], name)

    across_scale = deform_potential.reshape(-1, 1, width)

    def run(chunk, previous, after=(), again=False):
        kind, start, count = CHUNKS[chunk]
        return solve(
            inverse_blocks, coupling_blocks, previous, start, count, kind == "late", again, after
        )

    def rise(value, name):
        return send(value, "energy", up, "up" + name)

    def fall(value, name):
        return send(value, "energy", down, "down" + name)

    def done(sigma, chunk, local, got, after=(), parts=None):
        kind, start, _ = CHUNKS[chunk]
        return finish(
            sigma,
            inverse_blocks.shape,
            start,
            across_scale,
            kind == "late",
            local,
            got,
            after,
            parts,
        )

    g0, n0, low0, high0 = run(0, None)
    up0, c0 = rise(high0, "0"), core(g0, "core0")
    g1, n1 = run(1, g0, (c0,))
    y1, c1 = pair(g1, "pair1"), core(g1, "core1")
    (low0,) = gate([low0], (g1,))
    down0 = fall(low0, "0")
    g3, n3, h3 = run(3, g1, (c1,), True)
    y3 = pair(g3, "pair3")
    g2, n2, low2, high2, h2 = run(2, g3, (), True)
    weights = own_weights(shifts, emission_weight, absorption_weight, (n2,))

    low2, high2, h2 = gate([low2, high2, h2], (weights,))
    up2, down2, c2 = rise(high2, "2"), fall(low2, "2"), core(h2, "core2")
    (n0,) = gate([n0], (low2,))

    up0, down0 = gate([up0, down0], (n0, c2))
    core_up0, core_down0 = core(up0, "core_up0"), core(down0, "core_down0")
    (c0,) = gate([c0], (up0,))
    y1, h3 = gate([y1, h3], (c0,))
    core_y1, c3 = core(y1, "core_pair1"), core(h3, "core3")
    (c1,) = gate([c1], (y1,))
    members1 = (g1, c1, y1, core_y1)
    high1, low1, local1 = early_edges(weights, members1, (c3,))
    high1, low1, n1 = gate([high1, low1, n1], ())
    up1, down1, beat1 = rise(high1, "1"), fall(low1, "1"), core(n1, "beat1")
    (n2,) = gate([n2], (n1,))

    members0 = (g0, c0, up0, down0, core_up0, core_down0)
    total0, local0 = late_sum(weights, members0, (n2,))
    x0 = pair(total0, "pair0")
    (n3,) = gate([n3], (total0, beat1))

    up2, down2 = gate([up2, down2], (n3,))
    core_up2, core_down2 = core(up2, "core_up2"), core(down2, "core_down2")
    (c2,) = gate([c2], (up2,))
    (y3,) = gate([y3], (c2, core_up2, core_down2))
    core_y3 = core(y3, "core_pair3")
    members2 = (g2, c2, up2, down2, core_up2, core_down2)
    total2, local2 = late_sum(weights, members2, (y3,))
    x2 = pair(total2, "pair2")

    members3 = (g3, c3, y3, core_y3)
    high3, low3, local3 = early_edges(weights, members3, (total2,))
    up3, down3 = rise(high3, "3"), fall(low3, "3")

    parts = range_parts(range_rows, [n0, n1, n3, n2], (low3,))
    received = lax.all_to_all(parts, ("energy", "mom"), split_axis=0, concat_axis=0, tiled=True)
    (sigma,) = done(None, 0, local0, (x0,), (parts,))
    (sigma,) = done(sigma, 1, local1, (up1, down1))
    (sigma,) = done(sigma, 3, local3, (up3, down3))
    sigma, charge = done(sigma, 2, local2, (x2,), (), received)
    return sigma, charge


def solution(mesh):
    in_specs = (
        P(None, "energy", "mom", None, None),
        P(None, "mom", None, None),
        P(),
        P(),
        P(),
        P(),
        P(),
    )
    out_specs = (P(None, "energy", "mom", None, None), P(("energy", "mom")))
    return jax.shard_map(body, mesh=mesh, in_specs=in_specs, out_specs=out_specs, check_vma=False)
```

```python
import functools

import jax
import jax.numpy as jnp
from jax import lax
from jax.experimental import pallas as pl
from jax.experimental.pallas import tpu as pltpu
from jax.sharding import PartitionSpec as P

CHUNKS = (("late", 0, 2), ("early", 2, 2), ("late", 6, 2), ("early", 4, 2))
VMEM = 63 * 2**20
TILE = 16
UNROLL = 16
ANY = pl.BlockSpec(memory_space=pltpu.HBM)
FACTOR = 100.0


def cost(us):
    return pl.CostEstimate(
        flops=int(us * FACTOR * 1.15e9), bytes_accessed=0, transcendentals=0
    )


F32 = jnp.float32
BF16 = jnp.bfloat16


def unread(values):
    return [ANY] * len(values)


def dot(left, right, transpose=False):
    dims = (((1,), (1 if transpose else 0,)), ((), ()))
    return lax.dot_general(left, right, dims, preferred_element_type=F32)


def complex_dot(left, right):
    wide = jnp.concatenate(left, axis=1)
    re = dot(wide, jnp.concatenate([right[0], -right[1]], axis=0))
    im = dot(wide, jnp.concatenate([right[1], right[0]], axis=0))
    return re.astype(BF16), im.astype(BF16)


def complex_dot_adjoint(left, right):
    wide = jnp.concatenate(left, axis=1)
    re = dot(wide, jnp.concatenate([right[0], right[1]], axis=1), True)
    im = dot(wide, jnp.concatenate([-right[1], right[0]], axis=1), True)
    return re.astype(BF16), im.astype(BF16)


def solve_kernel(first, edges, again, *refs):
    refs = list(refs)
    a_ref, t_ref = refs[:2]
    previous_ref = None if first else refs[2]
    carry = refs.pop()
    again_ref = refs.pop() if again else None
    low_ref, high_ref = refs[-2:] if edges else (None, None)
    outs = refs[:-2] if edges else refs
    green_ref, density_ref = outs[-2:]
    energies = a_ref.shape[1]
    width = a_ref.shape[-1]
    t = (t_ref[0, 0], t_ref[1, 0])
    odd = lax.rem(lax.axis_index("energy"), 2)
    if not first:

        @pl.when(pl.program_id(0) == 0)
        def _():
            carry[...] = previous_ref[0]

    rows = lax.broadcasted_iota(jnp.int32, (width, width), 0)
    columns = lax.broadcasted_iota(jnp.int32, (width, width), 1)
    total = jnp.zeros((8, width), F32)
    if first:

        @pl.when(pl.program_id(0) == 0)
        def _():
            couple = complex_dot_adjoint(t, t)
            for e in range(energies):
                carry[0, e], carry[1, e] = couple

        @pl.when(pl.program_id(0) > 0)
        def _():
            for e in range(energies):
                left = complex_dot(t, (carry[0, e], carry[1, e]))
                carry[0, e], carry[1, e] = complex_dot_adjoint(left, t)

    blocks = [(a_ref[0, e, 0], a_ref[1, e, 0]) for e in range(energies)]
    couples = [(carry[0, e], carry[1, e]) for e in range(energies)]
    if not first:
        lefts = [complex_dot(t, green) for green in couples]
        couples = [complex_dot_adjoint(left, t) for left in lefts]
    inners = [complex_dot(a, couple) for a, couple in zip(blocks, couples)]
    for e in range(energies):
        a, inner = blocks[e], inners[e]
        wide = jnp.concatenate(inner, axis=1)
        re = a[0].astype(F32) + dot(wide, jnp.concatenate([a[0], -a[1]], axis=0))
        im = a[1].astype(F32) + dot(wide, jnp.concatenate([a[1], a[0]], axis=0))
        re, im = re.astype(BF16), im.astype(BF16)
        carry[0, e] = re
        carry[1, e] = im
        green_ref[0, 0, e] = re
        green_ref[0, 1, e] = im
        if again:
            again_ref[0, 0, e] = re
            again_ref[0, 1, e] = im
        for low in [edge for edge, at in ((True, 0), (False, energies - 1)) if edges and e == at]:
            for parity, target in ((1, low_ref if low else high_ref), (0, high_ref if low else low_ref)):

                @pl.when(odd == parity)
                def _(target=target, re=re, im=im):
                    target[0, 0] = re
                    target[0, 1] = im
        diagonal = jnp.where(rows == columns, im.astype(F32), 0.0)
        total = total + jnp.sum(diagonal.reshape(width // 8, 8, width), axis=0)
    density_ref[0] = total


def solve(inverse, coupled, previous, start, count, edges, again, after=()):
    _, energies, _, total_rows, width = inverse.shape
    first = previous is None
    args = [inverse, coupled]
    in_specs = [
        pl.BlockSpec((2, energies, 1, width, width), lambda i: (0, 0, 0, start + i, 0)),
        pl.BlockSpec((2, 1, width, width), lambda i: (0, 0, start + i, 0)),
    ]
    if not first:
        last = previous.shape[0] - 1
        args.append(previous)
        in_specs.append(
            pl.BlockSpec((1, 2, energies, width, width), lambda i: (last, 0, 0, 0, 0))
        )
    args.extend(after)
    in_specs.extend(unread(after))
    out_shape = [
        jax.ShapeDtypeStruct((count, 2, energies, width, width), BF16),
        jax.ShapeDtypeStruct((count, 8, width), F32),
    ]
    out_specs = [
        pl.BlockSpec((1, 2, energies, width, width), lambda i: (i, 0, 0, 0, 0)),
        pl.BlockSpec((1, 8, width), lambda i: (i, 0, 0)),
    ]
    if edges:
        for _ in range(2):
            out_shape.append(jax.ShapeDtypeStruct((count, 2, width, width), BF16))
            out_specs.append(pl.BlockSpec((1, 2, width, width), lambda i: (i, 0, 0, 0)))
    if again:
        out_shape.append(out_shape[0])
        out_specs.append(out_specs[0])
    return pl.pallas_call(
        functools.partial(solve_kernel, first, edges, again),
        grid=(count,),
        in_specs=in_specs,
        out_specs=out_specs,
        out_shape=out_shape,
        scratch_shapes=[pltpu.VMEM((2, energies, width, width), BF16)],
        compiler_params=pltpu.CompilerParams(vmem_limit_bytes=VMEM),
        cost_estimate=cost(2.5 * count),
        name="solve",
    )(*args)


def grid_spec(energies, width):
    return pl.BlockSpec((1, 2, energies, width, width), lambda i: (i, 0, 0, 0, 0))


def edge_spec(width):
    return pl.BlockSpec((1, 2, width, width), lambda i: (i, 0, 0, 0))


def gate_kernel(*refs):
    pass


def gate(values, after):
    count = len(values)
    return pl.pallas_call(
        gate_kernel,
        in_specs=[ANY] * count + unread(after),
        out_specs=[ANY] * count,
        out_shape=[jax.ShapeDtypeStruct(value.shape, value.dtype) for value in values],
        input_output_aliases={i: i for i in range(count)},
        compiler_params=pltpu.CompilerParams(vmem_limit_bytes=VMEM),
        cost_estimate=cost(2.0),
        name="gate",
    )(*values, *after)


def tiles(width):
    steps = width // TILE

    def run(step_body):
        for part in range(2):

            @pl.loop(0, steps, unroll=UNROLL)
            def _(step):
                step_body(part, pl.ds(pl.multiple_of(step * TILE, TILE), TILE))

    return run


def weighted(terms):
    total = None
    for weight, value in terms:
        term = value if weight is None else weight * value
        total = term if total is None else total + term
    return total


def early_edges_kernel(w_ref, *refs):
    grids, (high_ref, low_ref, local_ref) = refs[:4], refs[-3:]
    energies, width = grids[0].shape[2:4]
    odd = lax.rem(lax.axis_index("energy"), 2) == 1
    w = [[w_ref[0, o, j] for j in range(4)] for o in range(3)]

    @tiles(width)
    def _(part, rows):
        line = [
            [ref[0, part, e, rows, :].astype(F32) for e in range(energies)] for ref in grids
        ]
        high = [(w[0][j], line[j][energies - 1]) for j in range(4)]
        low = [(w[2][j], line[j][0]) for j in range(4)]
        high, low = weighted(high), weighted(low)
        high_ref[0, part, rows, :] = jnp.where(odd, high, low).astype(BF16)
        low_ref[0, part, rows, :] = jnp.where(odd, low, high).astype(BF16)
        for e in range(energies):
            terms = [
                (w[o][j], line[j][e + o - 1])
                for j in range(4)
                for o in range(3)
                if 0 <= e + o - 1 < energies
            ]
            local_ref[0, part, e, rows, :] = weighted(terms).astype(BF16)


def early_edges(weights, members, after):
    count, _, energies, width, _ = members[0].shape
    edge = jax.ShapeDtypeStruct((count, 2, width, width), BF16)
    spec = grid_spec(energies, width)
    return pl.pallas_call(
        early_edges_kernel,
        grid=(count,),
        in_specs=[pl.BlockSpec(memory_space=pltpu.SMEM)] + [spec] * 4 + unread(after),
        out_specs=[edge_spec(width)] * 2 + [spec],
        out_shape=[edge, edge, jax.ShapeDtypeStruct(members[0].shape, BF16)],
        compiler_params=pltpu.CompilerParams(vmem_limit_bytes=VMEM),
        cost_estimate=cost(1.7 * count),
        name="early_edges",
    )(weights, *members, *after)


def late_line(refs, part, rows):
    grids, edges = refs[:2], refs[2:]
    lines = []
    odd = lax.rem(lax.axis_index("energy"), 2) == 1
    for j in range(2):
        near = edges[2 * j + 1][0, part, rows, :].astype(F32)
        far = edges[2 * j][0, part, rows, :].astype(F32)
        line = [jnp.where(odd, near, far)]
        line += [
            grids[j][0, part, e, rows, :].astype(F32) for e in range(grids[j].shape[2])
        ]
        line += [jnp.where(odd, far, near)]
        lines.append(line)
    return lines


def late_sum_kernel(w_ref, *refs):
    members, outs = refs[:6], refs[-2:]
    energies, width = members[0].shape[2:4]
    w = [[[w_ref[t, o, j] for j in range(2)] for o in range(3)] for t in range(2)]

    @tiles(width)
    def _(part, rows):
        line = late_line(members, part, rows)
        for target, out_ref in zip((1, 0), outs):
            for e in range(energies):
                terms = [(w[target][o][j], line[j][e + o]) for j in range(2) for o in range(3)]
                out_ref[0, part, e, rows, :] = weighted(terms).astype(BF16)


def late_sum(weights, members, after):
    count, _, energies, width, _ = members[0].shape
    spec = grid_spec(energies, width)
    return pl.pallas_call(
        late_sum_kernel,
        grid=(count,),
        in_specs=[pl.BlockSpec(memory_space=pltpu.SMEM)]
        + [spec] * 2
        + [edge_spec(width)] * 4
        + unread(after),
        out_specs=[spec, spec],
        out_shape=[jax.ShapeDtypeStruct(members[0].shape, BF16)] * 2,
        compiler_params=pltpu.CompilerParams(vmem_limit_bytes=VMEM),
        cost_estimate=cost(1.8 * count),
        name="late_sum",
    )(weights, *members, *after)


def finish_kernel(late, charged, across_ref, local_ref, *refs):
    received = refs[:1] if late else refs[:2]
    out_ref, down_ref = refs[-3 if charged else -2], refs[-1]
    if charged:
        parts_ref, charge_ref = refs[len(received)], refs[-2]

        @pl.when(pl.program_id(0) == 0)
        def _():
            charge_ref[0] = jnp.sum(parts_ref[...])

    energies, width = local_ref.shape[2:4]
    across = across_ref[0]
    lanes = down_ref.shape[1]
    odd = lax.rem(lax.axis_index("energy"), 2) == 1
    down_ref[...] = jnp.transpose(jnp.broadcast_to(across, (lanes, width)))

    @tiles(width)
    def _(part, rows):
        if not late:
            far, near = [ref[0, part, rows, :].astype(F32) for ref in received]
            before, behind = jnp.where(odd, near, far), jnp.where(odd, far, near)
        scale = jnp.concatenate([down_ref[rows, :]] * (width // lanes), axis=1) * across
        for e in range(energies):
            total = local_ref[0, part, e, rows, :].astype(F32)
            if late:
                total = total + received[0][0, part, e, rows, :].astype(F32)
            if not late and e == 0:
                total = total + before
            if not late and e == energies - 1:
                total = total + behind
            out_ref[part, e, 0, rows, :] = (total * scale).astype(BF16)


def finish(sigma, shape, start, across, late, local, received, after, parts):
    count, _, energies, width, _ = local.shape
    args = [across, local, *received]
    in_specs = [
        pl.BlockSpec((1, 1, width), lambda i: (start + i, 0, 0)),
        grid_spec(energies, width),
    ]
    in_specs += [grid_spec(energies, width)] if late else [edge_spec(width)] * 2
    out_shape = [jax.ShapeDtypeStruct(shape, BF16)]
    out_specs = [
        pl.BlockSpec((2, energies, 1, width, width), lambda i: (0, 0, 0, start + i, 0))
    ]
    if parts is not None:
        args.append(parts)
        in_specs.append(pl.BlockSpec(parts.shape, lambda i: (0,) * parts.ndim))
        out_shape.append(jax.ShapeDtypeStruct((1,), F32))
        out_specs.append(pl.BlockSpec(memory_space=pltpu.SMEM))
    args += after
    in_specs += unread(after)
    aliases = {}
    if sigma is not None:
        aliases = {len(args): 0}
        args.append(sigma)
        in_specs.append(ANY)
    return pl.pallas_call(
        functools.partial(finish_kernel, late, parts is not None),
        grid=(count,),
        in_specs=in_specs,
        out_specs=out_specs,
        out_shape=out_shape,
        input_output_aliases=aliases,
        scratch_shapes=[pltpu.VMEM((width, 128), F32)],
        compiler_params=pltpu.CompilerParams(vmem_limit_bytes=VMEM),
        cost_estimate=cost(2.2 * count),
        name="finish",
    )(*args)


def range_parts_kernel(count, range_ref, *refs):
    densities, out_ref = refs[:count], refs[-1]
    width = densities[0].shape[-1]
    lanes = lax.broadcasted_iota(jnp.int32, (8, 128), 1)
    pieces = []
    base = 0
    for ref in densities:
        for i in range(ref.shape[0]):
            for half in range(width // 128):
                pieces.append((base, ref[i, :, half * 128 : (half + 1) * 128]))
                base += 128

    def one_range(d, begin):
        end = begin + range_ref[d]
        total = jnp.zeros((8, 128), F32)
        for offset, value in pieces:
            inside = (lanes >= begin - offset) & (lanes < end - offset)
            total = total + jnp.where(inside, value, 0.0)
        out_ref[d] = -jnp.sum(total, axis=0, keepdims=True)
        return end

    lax.fori_loop(0, out_ref.shape[0], one_range, jnp.int32(0), unroll=4)


def range_parts(range_rows, densities, after):
    devices = range_rows.shape[0]
    return pl.pallas_call(
        functools.partial(range_parts_kernel, len(densities)),
        in_specs=[pl.BlockSpec(memory_space=pltpu.SMEM)]
        + [pl.BlockSpec(memory_space=pltpu.VMEM)] * len(densities)
        + unread(after),
        out_specs=pl.BlockSpec(memory_space=pltpu.VMEM),
        out_shape=jax.ShapeDtypeStruct((devices, 1, 128), F32),
        compiler_params=pltpu.CompilerParams(vmem_limit_bytes=VMEM),
        cost_estimate=cost(2.2),
        name="range_parts",
    )(range_rows, *densities, *after)


def own_weights_kernel(shift_ref, emission_ref, absorption_ref, *refs):
    out_ref = refs[-1]
    me = lax.axis_index("mom")
    zero = jnp.float32(0)
    for target in range(2):
        for offset in (-1, 0, 1):
            for j in range(4):
                total = zero
                for p in range(shift_ref.shape[0]):
                    emitted = emission_ref[p, me ^ (2 * target), me ^ j]
                    absorbed = absorption_ref[p, me ^ (2 * target), me ^ j]
                    total = total + jnp.where(shift_ref[p] == -offset, emitted, zero)
                    total = total + jnp.where(shift_ref[p] == offset, absorbed, zero)
                out_ref[target, offset + 1, j] = total


def own_weights(shifts, emission, absorption, after):
    smem = pl.BlockSpec(memory_space=pltpu.SMEM)
    return pl.pallas_call(
        own_weights_kernel,
        in_specs=[smem] * 3 + unread(after),
        out_specs=smem,
        out_shape=jax.ShapeDtypeStruct((2, 3, 4), F32),
        compiler_params=pltpu.CompilerParams(vmem_limit_bytes=VMEM),
        cost_estimate=cost(0.5),
        name="own_weights",
    )(shifts, emission, absorption, *after)


def body(
    inverse_blocks,
    coupling_blocks,
    shifts,
    emission_weight,
    absorption_weight,
    deform_potential,
    range_rows,
):
    n_energy = lax.axis_size("energy")
    width = inverse_blocks.shape[-1]
    between = [(i, i + 1) for i in range(1, n_energy - 1, 2)]
    up = between + [(j, i) for i, j in between]
    down = [(i, i ^ 1) for i in range(n_energy)]

    def send(value, axis, pairs, name):
        with jax.named_scope(name):
            return lax.ppermute(value, axis, pairs)

    def core(value, name):
        return send(value, "mom", [(i, i ^ 1) for i in range(4)], name)

    def pair(value, name):
        return send(value, "mom", [(i, i ^ 2) for i in range(4)], name)

    across_scale = deform_potential.reshape(-1, 1, width)

    def run(chunk, previous, after=(), again=False):
        kind, start, count = CHUNKS[chunk]
        return solve(
            inverse_blocks, coupling_blocks, previous, start, count, kind == "late", again, after
        )

    def rise(value, name):
        return send(value, "energy", up, "up" + name)

    def fall(value, name):
        return send(value, "energy", down, "down" + name)

    def done(sigma, chunk, local, got, after=(), parts=None):
        kind, start, _ = CHUNKS[chunk]
        return finish(
            sigma,
            inverse_blocks.shape,
            start,
            across_scale,
            kind == "late",
            local,
            got,
            after,
            parts,
        )

    g0, n0, low0, high0 = run(0, None)
    down0, c0 = fall(low0, "0"), core(g0, "core0")
    g1, n1 = run(1, g0, (c0,))
    y1, c1 = pair(g1, "pair1"), core(g1, "core1")
    (high0,) = gate([high0], (g1,))
    up0 = rise(high0, "0")
    g3, n3, h3 = run(3, g1, (c1,), True)
    y3 = pair(g3, "pair3")
    g2, n2, low2, high2, h2 = run(2, g3, (), True)
    weights = own_weights(shifts, emission_weight, absorption_weight, (n2,))

    low2, high2, h2 = gate([low2, high2, h2], (n2,))
    up2, down2, c2 = rise(high2, "2"), fall(low2, "2"), core(h2, "core2")
    (n0,) = gate([n0], (low2,))

    up0, down0 = gate([up0, down0], (n0, c2))
    core_up0, core_down0 = core(up0, "core_up0"), core(down0, "core_down0")
    (c0,) = gate([c0], (up0,))
    y1, h3 = gate([y1, h3], (c0,))
    core_y1, c3 = core(y1, "core_pair1"), core(h3, "core3")
    (c1,) = gate([c1], (y1,))
    members1 = (g1, c1, y1, core_y1)
    high1, low1, local1 = early_edges(weights, members1, (c3,))
    high1, low1, n1 = gate([high1, low1, n1], ())
    up1, down1, beat1 = rise(high1, "1"), fall(low1, "1"), core(n1, "beat1")
    (n2,) = gate([n2], (n1,))

    members0 = (g0, c0, up0, down0, core_up0, core_down0)
    total0, local0 = late_sum(weights, members0, (n2,))
    x0 = pair(total0, "pair0")
    (n3,) = gate([n3], (total0, beat1))

    up2, down2 = gate([up2, down2], (n3,))
    core_up2, core_down2 = core(up2, "core_up2"), core(down2, "core_down2")
    (c2,) = gate([c2], (up2,))
    (y3,) = gate([y3], (c2, core_up2, core_down2))
    core_y3 = core(y3, "core_pair3")
    members2 = (g2, c2, up2, down2, core_up2, core_down2)
    total2, local2 = late_sum(weights, members2, (y3,))
    x2 = pair(total2, "pair2")

    members3 = (g3, c3, y3, core_y3)
    high3, low3, local3 = early_edges(weights, members3, (total2,))
    up3, down3 = rise(high3, "3"), fall(low3, "3")

    parts = range_parts(range_rows, [n0, n1, n3, n2], (low3,))
    received = lax.all_to_all(parts, ("energy", "mom"), split_axis=0, concat_axis=0, tiled=True)
    (sigma,) = done(None, 0, local0, (x0,), (parts,))
    (sigma,) = done(sigma, 1, local1, (up1, down1))
    (sigma,) = done(sigma, 3, local3, (up3, down3))
    sigma, charge = done(sigma, 2, local2, (x2,), (), received)
    return sigma, charge


def solution(mesh):
    in_specs = (
        P(None, "energy", "mom", None, None),
        P(None, "mom", None, None),
        P(),
        P(),
        P(),
        P(),
        P(),
    )
    out_specs = (P(None, "energy", "mom", None, None), P(("energy", "mom")))
    return jax.shard_map(body, mesh=mesh, in_specs=in_specs, out_specs=out_specs, check_vma=False)
```
